256 devices in a mesh: layer: 4 (over x), prow: 8 (over z), pcol: 8 (over y, core).
Axes of the slice: x: 4, y: 4, z: 8, core: 2. Of those that a mesh axis runs over, the one named last changes fastest.
Arguments:
- separator: float32 [8192, 8192], P('prow', 'pcol'), may hold values from -6 to 6
- left_factor: bfloat16 [16384, 128, 128], P(('layer', 'prow', 'pcol')), may hold values from -6 to 6
- right_factor: bfloat16 [16384, 128, 128], P(('layer', 'prow', 'pcol')), may hold values from -0.5 to 0.5
- owners: int32 [16384, 1], P(('layer', 'prow', 'pcol')), may hold values from 0 to 63; in each aligned block of 64 rows (0 to 63, 64 to 127, ...) at most 2 rows name the same one
- spots: int32 [16384], P(('layer', 'prow', 'pcol')), may hold values from 0 to 63
- pivot_order: int32 [512], replicated, may hold values from 0 to 511, each once
- panel_inverses: bfloat16 [512, 512], replicated, may hold values from -0.2 to 0.2
Outputs:
- factored: float32 [8192, 8192], P('prow', 'pcol')
The draws below stay inside these ranges and needn't reach their ends.
Inputs may be any that keep to these rules, and one draw needn't show every extreme that they name: `owners`: of the 64 update blocks of one device, at most 2 name the same owner.
All inputs are finite; a program needn't handle non-finite values.
Results may differ from the reference program's by a relative error of at most 0.0003.
Values sent between devices are 32-bit elements; how exact they have to be, the bound alone decides.
A program may use at most 128 MiB of HBM per device.

```python
import math
import jax
import jax.numpy as jnp
import numpy as np
from jax import lax

SEP = 8192
PANEL = 512
BLOCK = 128
SUPER = 128
UPD_DEV = 64
OWNERS = 64
CAP = 2
UPDATES = 16384
PIECE_ROWS = 1024
PIECE_COLS = 1024
PIECE_BLOCKS = 64
N_PCOL = 8


def draw_panel_inverses(key, part):
    key = jax.random.fold_in(key, 5)
    first_key, second_key = jax.random.split(key, 2)
    noise = jax.random.truncated_normal(first_key, -4.0, 4.0, (PANEL, PANEL), jnp.float32)
    diagonal = jnp.exp(jax.random.uniform(second_key, (PANEL, 1), jnp.float32, math.log(0.02), math.log(0.08)))
    factor = PANEL ** (-0.5)
    row_index = jnp.arange(PANEL)[:, None]
    col_index = jnp.arange(PANEL)[None, :]
    lower_part = jnp.clip(noise * factor, -0.199, 0.199)
    upper_part = jnp.clip(noise * (0.03 * factor), -0.199, 0.199)
    result = jnp.where(row_index > col_index, lower_part, jnp.where(row_index == col_index, diagonal, upper_part))
    return result.astype(jnp.bfloat16)


def set_ends(array, rng, smallest, largest):
    longest = array.shape.index(max(array.shape))
    spots = []
    for shift in (0, 1):
        where = [jax.random.randint(jax.random.fold_in(rng, axis), (), 0, length) for axis, length in enumerate(array.shape)]
        where[longest] = (where[longest] + shift) % array.shape[longest]
        spots.append(tuple(where))
    return array.at[spots[0]].set(smallest).at[spots[1]].set(largest)


def steps_of(own_key, extent, cuts, smallest, largest):
    loudness, own = 1.0, jax.random.fold_in(own_key, 6)
    for position, blocks in cuts:
        steps = jnp.exp(jax.random.uniform(jax.random.fold_in(own, position), (blocks,), jnp.float32, smallest / len(cuts), largest / len(cuts)))
        loudness = loudness * jnp.repeat(steps, extent[position] // blocks).reshape([-1 if axis == position else 1 for axis in range(len(extent))])
    return loudness


def shared_out(own_key, own, number, rows, amount, top, bound, slope):
    sequence = jax.random.permutation(own_key, amount)
    crowded, ordinary = load_shares(amount, rows * top, bound, slope, True), load_shares(amount, rows * top, bound, slope, False)
    places = jnp.arange(amount)

    def named(lengths, rotation):
        used = int((lengths > 0).sum())
        fixed = max(1, used // 4)
        shifted = fixed + (places - fixed + rotation * (used - fixed)) % max(1, amount - fixed)
        return jnp.zeros((amount,), jnp.int32).at[sequence[jnp.where(places < fixed, places, shifted)]].set(jnp.asarray(lengths, jnp.int32))

    lengths = jnp.where(number % 4 == 0, named(crowded, number // 4), named(ordinary, number - number // 4 - 1))
    mixed = jax.random.permutation(jax.random.fold_in(own, 3), amount)
    source_of, sink = mixed[0:amount // 2 * 2:2], mixed[1:amount // 2 * 2:2]
    margin = jnp.minimum(lengths[source_of] - 1, bound - lengths[sink]) // 2
    margin = jnp.where((source_of == sequence[0]) | (sink == sequence[0]) | (lengths[sink] == 0), 0, jnp.maximum(margin, 0))
    shifted = jax.random.randint(jax.random.fold_in(own, 4), (amount // 2,), 0, 1 << 20) % (margin + 1)
    lengths = lengths.at[source_of].add(-shifted).at[sink].add(shifted)
    items = jnp.searchsorted(jnp.cumsum(lengths), jnp.arange(rows * top), side="right").astype(jnp.int32)
    table = items.reshape(top, rows).T
    table = table[jax.random.permutation(jax.random.fold_in(own, 1), rows)]
    rotation = jax.random.randint(jax.random.fold_in(own, 2), (rows, 1), 0, top)
    return jnp.take_along_axis(table, (jnp.arange(top)[None, :] + rotation) % top, axis=1)


def load_shares(count, total, bound, skew, full):
    portions = [(1 << 20) // math.isqrt(rank ** skew) + 1 for rank in range(1, count + 1)]
    largest = bound if full else min(bound, max(-(-total // count), total * portions[0] // sum(portions)))
    least = 1 if total - largest >= count - 1 else 0
    given, spare = [largest] + [least] * (count - 1), total - largest - least * (count - 1)
    while spare > 0:
        free = [i for i in range(1, count) if given[i] < largest] or [i for i in range(1, count) if given[i] < bound]
        pool, left = sum([portions[i] for i in free]), spare
        for i in free:
            extra = min(bound - given[i], max(1, left * portions[i] // pool), spare)
            given[i] = given[i] + extra
            spare = spare - extra
    return np.array(given)


def scatter_about(stream_key, shape, deviation, reach, cuts=(), kind=jnp.bfloat16):
    values = deviation * jax.random.normal(stream_key, shape, jnp.float32)
    if cuts:
        values = values * steps_of(stream_key, shape, cuts, -0.22, 0.18)
    return jnp.clip(values, -reach, reach).astype(kind)


def setup_inputs(seed: int = 0) -> dict:
    keys = jax.random.split(jax.random.key(seed), 8)
    separator = scatter_about(keys[0], (SEP, SEP), 1.0, 6.0, ((0, 8), (1, 8)), jnp.float32)
    left_factor = scatter_about(keys[1], (UPDATES, BLOCK, SUPER), 1.0, 6.0, ((0, 256),))
    right_factor = scatter_about(keys[2], (UPDATES, SUPER, BLOCK), SUPER ** -0.5, 0.5, ((0, 256),))
    owners_keys = jax.random.split(jax.random.fold_in(keys[3], 1), UPDATES // UPD_DEV)
    owners_turns = jax.random.permutation(jax.random.fold_in(keys[3], 3), UPDATES // UPD_DEV)
    owners = jax.vmap(lambda own, number: shared_out(jax.random.fold_in(keys[3], 2), own, number, UPD_DEV, OWNERS, 1, CAP, 0))(owners_keys, owners_turns).reshape((UPDATES, 1))
    spots = set_ends(jax.random.randint(keys[4], (UPDATES,), 0, PIECE_BLOCKS), jax.random.fold_in(keys[4], 1), 0, PIECE_BLOCKS - 1).astype(jnp.int32)
    pivot_order = jax.random.permutation(keys[5], PANEL).astype(jnp.int32)
    panel_inverses = draw_panel_inverses(jax.random.fold_in(keys[7], 71), 0)
    return dict(separator=separator, left_factor=left_factor, right_factor=right_factor, owners=owners, spots=spots, pivot_order=pivot_order, panel_inverses=panel_inverses)


def reference(separator, left_factor, right_factor, owners, spots, pivot_order, panel_inverses):
    per_row = PIECE_ROWS // BLOCK
    per_col = PIECE_COLS // BLOCK
    groups = UPDATES // UPD_DEV
    destination = owners[:, 0].astype(jnp.int32)
    block_rows = ((destination // N_PCOL) * per_row + spots // per_col).astype(jnp.int32)
    block_cols = ((destination % N_PCOL) * per_col + spots % per_col).astype(jnp.int32)

    def accumulate(running, pieces):
        left_group, right_group, rows_here, cols_here = pieces
        products = jnp.einsum("uab,ubc->uac", left_group.astype(jnp.float32), right_group.astype(jnp.float32), precision=lax.Precision.HIGHEST)
        return running.at[rows_here, cols_here].add(products), None

    shaped = (left_factor.reshape(groups, UPD_DEV, BLOCK, SUPER), right_factor.reshape(groups, UPD_DEV, SUPER, BLOCK), block_rows.reshape(groups, UPD_DEV), block_cols.reshape(groups, UPD_DEV))
    initial = jnp.zeros((SEP // BLOCK, SEP // BLOCK, BLOCK, BLOCK), jnp.float32)
    summed, _ = lax.scan(accumulate, initial, shaped)
    contributions = summed.transpose(0, 2, 1, 3).reshape(SEP, SEP)
    reduced = separator - contributions
    permuted_top = reduced[pivot_order.astype(jnp.int32)]
    inverses = panel_inverses.astype(jnp.float32)
    lower_inverse = jnp.tril(inverses, -1) + jnp.eye(PANEL, dtype=jnp.float32)
    upper_inverse = jnp.triu(inverses)
    upper_panel = jnp.dot(lower_inverse, permuted_top[:, PANEL:], precision=lax.Precision.HIGHEST)
    lower_panel = jnp.dot(reduced[PANEL:, :PANEL], upper_inverse, precision=lax.Precision.HIGHEST)
    trailing = reduced[PANEL:, PANEL:] - jnp.dot(lower_panel, upper_panel, precision=lax.Precision.HIGHEST)
    head_rows = jnp.concatenate([permuted_top[:, :PANEL], upper_panel], axis=1)
    tail_rows = jnp.concatenate([lower_panel, trailing], axis=1)
    return jnp.concatenate([head_rows, tail_rows], axis=0)
```

```python
import functools

import jax
import jax.numpy as jnp
from jax import lax
from jax.experimental import pallas as pl
from jax.experimental.pallas import tpu as pltpu
from jax.sharding import PartitionSpec as P

MESH = pl.DeviceIdType.MESH
GRID = 8
OWNERS = GRID * GRID
BLOCK = 128
F32 = jnp.float32


def broadcast(x, axis, root):
    mine = lax.axis_index(axis) == root
    return lax.psum(jnp.where(mine, x, jnp.zeros_like(x)), axis)


def exchange_kernel(index_ref, left_ref, right_ref, recv_ref, out_buf, send_sem, recv_sem, own_sem):
    layer, row, col = lax.axis_index("layer"), lax.axis_index("prow"), lax.axis_index("pcol")
    me = row * GRID + col

    def place(k):
        r = (row + k % GRID) % GRID
        c = (col + k // GRID) % GRID
        return r, c

    barrier = pltpu.get_barrier_semaphore()

    def greet(k, carry):
        r, c = place(k)
        pl.semaphore_signal(barrier, inc=1, device_id=(layer, r, c), device_id_type=MESH)
        return carry

    lax.fori_loop(1, OWNERS, greet, 0)

    def product(k):
        r, c = place(k)
        u = index_ref[r * GRID + c]
        out_buf[k] = jnp.dot(left_ref[u], right_ref[u], preferred_element_type=F32)

    def copy(k):
        r, c = place(k)
        return pltpu.make_async_remote_copy(
            src_ref=out_buf.at[k],
            dst_ref=recv_ref.at[me],
            send_sem=send_sem.at[k],
            recv_sem=recv_sem.at[k],
            device_id=(layer, r, c),
            device_id_type=MESH,
        )

    pl.semaphore_wait(barrier, OWNERS - 1)

    def send(k, carry):
        product(k)
        copy(k).start()
        return carry

    lax.fori_loop(1, OWNERS, send, 0)
    product(0)
    own = pltpu.make_async_copy(out_buf.at[0], recv_ref.at[me], own_sem)
    own.start()
    own.wait()

    def finish(k, carry):
        copy(k).wait()
        return carry

    lax.fori_loop(1, OWNERS, finish, 0)


def exchange(index, left, right):
    return pl.pallas_call(
        exchange_kernel,
        out_shape=jax.ShapeDtypeStruct((OWNERS, BLOCK, BLOCK), F32),
        in_specs=[
            pl.BlockSpec(memory_space=pltpu.SMEM),
            pl.BlockSpec(memory_space=pltpu.VMEM),
            pl.BlockSpec(memory_space=pltpu.VMEM),
        ],
        out_specs=pl.BlockSpec(memory_space=pl.ANY),
        scratch_shapes=[
            pltpu.VMEM((OWNERS, BLOCK, BLOCK), F32),
            pltpu.SemaphoreType.DMA((OWNERS,)),
            pltpu.SemaphoreType.DMA((OWNERS,)),
            pltpu.SemaphoreType.DMA,
        ],
        compiler_params=pltpu.CompilerParams(
            collective_id=0, has_side_effects=True, vmem_limit_bytes=32 * 1024 * 1024
        ),
        cost_estimate=pl.CostEstimate(
            flops=2 * OWNERS * BLOCK**3, bytes_accessed=16 * 1024 * 1024, transcendentals=0
        ),
    )(index, left, right)


def scatter_kernel(per_step, spot_ref, extra_ref, recv_ref, extra_hbm, out_ref, extra_buf, extra_sem):
    step = pl.program_id(0)

    @pl.when(step == 0)
    def _():
        out_ref[...] = jnp.zeros_like(out_ref)

    def add(k, carry):
        spot = spot_ref[step * per_step + k]

        @pl.when(spot < 64)
        def _():
            slot = (spot % 8) * 8 + spot // 8
            out_ref[slot] += recv_ref[k]

        return carry

    lax.fori_loop(0, per_step, add, 0)

    def add_extra(k, carry):
        spot = extra_ref[step * per_step + k]

        @pl.when(spot < 64)
        def _():
            fetch = pltpu.make_async_copy(extra_hbm.at[step * per_step + k], extra_buf, extra_sem)
            fetch.start()
            fetch.wait()
            slot = (spot % 8) * 8 + spot // 8
            out_ref[slot] += extra_buf[...]

        return carry

    lax.fori_loop(0, per_step, add_extra, 0)


def scatter(spots, extra_spots, recv, extra):
    per_step = 8
    return pl.pallas_call(
        functools.partial(scatter_kernel, per_step),
        out_shape=jax.ShapeDtypeStruct((64, BLOCK, BLOCK), F32),
        grid=(OWNERS // per_step,),
        in_specs=[
            pl.BlockSpec(memory_space=pltpu.SMEM),
            pl.BlockSpec(memory_space=pltpu.SMEM),
            pl.BlockSpec((per_step, BLOCK, BLOCK), lambda i: (i, 0, 0)),
            pl.BlockSpec(memory_space=pl.ANY),
        ],
        out_specs=pl.BlockSpec((64, BLOCK, BLOCK), lambda i: (0, 0, 0)),
        scratch_shapes=[pltpu.VMEM((BLOCK, BLOCK), F32), pltpu.SemaphoreType.DMA],
        compiler_params=pltpu.CompilerParams(vmem_limit_bytes=24 * 1024 * 1024),
    )(spots, extra_spots, recv, extra)


def scatter_extra_kernel(extra_ref, dense_ref, extra_ref_data, out_ref):
    out_ref[...] = dense_ref[...]

    def add(k, carry):
        spot = extra_ref[k]

        @pl.when(spot < 64)
        def _():
            slot = (spot % 8) * 8 + spot // 8
            out_ref[slot] += extra_ref_data[k]

        return carry

    lax.fori_loop(0, OWNERS, add, 0)


def scatter_extra(extra_spots, dense, extra):
    return pl.pallas_call(
        scatter_extra_kernel,
        out_shape=jax.ShapeDtypeStruct((64, BLOCK, BLOCK), F32),
        in_specs=[
            pl.BlockSpec(memory_space=pltpu.SMEM),
            pl.BlockSpec(memory_space=pltpu.VMEM),
            pl.BlockSpec(memory_space=pltpu.VMEM),
        ],
        out_specs=pl.BlockSpec(memory_space=pltpu.VMEM),
        compiler_params=pltpu.CompilerParams(vmem_limit_bytes=24 * 1024 * 1024),
    )(extra_spots, dense, extra)


def local_sum(left, right, owners, spots):
    update_count = left.shape[0]
    most = update_count // 2
    destination = owners[:, 0]
    counter = jnp.arange(update_count)
    same = destination[:, None] == destination[None, :]
    rank = jnp.sum(same & (counter[None, :] < counter[:, None]), axis=1)
    named = (destination[None, :] == jnp.arange(OWNERS)[:, None]) & (rank == 0)[None, :]
    index = jnp.sum(jnp.where(named, counter[None, :], 0), axis=1)
    first_spot = jnp.sum(jnp.where(named, spots[None, :], 0), axis=1)
    first_spot = jnp.where(jnp.any(named, axis=1), first_spot, 64)
    second = rank == 1
    order = jnp.sum(second[None, :] & (counter[None, :] < counter[:, None]), axis=1)
    picked = second[None, :] & (order[None, :] == jnp.arange(most)[:, None])
    extra_index = jnp.sum(jnp.where(picked, counter[None, :], 0), axis=1)
    extra_code = jnp.sum(jnp.where(picked, destination[None, :] * 64 + spots[None, :], 0), axis=1)
    extra_code = jnp.where(jnp.any(picked, axis=1), extra_code, -1)
    table = jnp.concatenate([first_spot, extra_code, jnp.zeros((32,), jnp.int32)])[None, :]
    table = lax.all_gather(table, ("layer", "prow", "pcol"), axis=0, tiled=True)
    me = lax.axis_index("prow") * GRID + lax.axis_index("pcol")
    layer_table = lax.dynamic_slice_in_dim(table, lax.axis_index("layer") * OWNERS, OWNERS, 0)
    my_spots = lax.dynamic_index_in_dim(layer_table, me, 1, keepdims=False)
    rounds = jnp.max(jnp.sum(table[:, OWNERS : OWNERS + most] >= 0, axis=1))

    def extra_round(k):
        u = extra_index[k]
        block = jnp.dot(left[u], right[u], preferred_element_type=F32)
        blocks = lax.all_gather(block[None], ("prow", "pcol"), axis=0, tiled=True)
        code = lax.dynamic_index_in_dim(layer_table, OWNERS + k, 1, keepdims=False)
        extra_spots = jnp.where((code >= 0) & (code // 64 == me), code % 64, 64)
        return extra_spots, blocks

    recv = exchange(index, left, right)
    extra_spots, blocks = extra_round(0)
    dense = scatter(my_spots, extra_spots, recv, blocks)

    def body(carry):
        k, dense = carry
        extra_spots, blocks = extra_round(k)
        return k + 1, scatter_extra(extra_spots, dense, blocks)

    return lax.while_loop(lambda carry: carry[0] < rounds, body, (jnp.int32(1), dense))[1]


def per_device(separator, left_factor, right_factor, owners, spots, pivot_order, panel_inverses):
    panel_width = pivot_order.shape[0]
    piece_rows, piece_cols = separator.shape
    dense = local_sum(left_factor, right_factor, owners, spots)
    dense = dense.reshape(8, piece_rows, BLOCK).transpose(1, 0, 2).reshape(piece_rows, piece_cols)
    reduced = separator - lax.psum(dense, "layer")
    top_rows = jnp.take(reduced[:panel_width], pivot_order, axis=0)
    left_block = reduced[:, :panel_width]
    inverses = panel_inverses.astype(jnp.float32)
    lower_inverse = jnp.tril(inverses, -1) + jnp.eye(panel_width, dtype=jnp.float32)
    upper_inverse = jnp.triu(inverses)
    upper_rows = broadcast(top_rows, "prow", 0)
    left_columns = broadcast(left_block, "pcol", 0)
    upper_part = jnp.dot(lower_inverse, upper_rows, precision=lax.Precision.HIGHEST)
    lower_part = jnp.dot(left_columns, upper_inverse, precision=lax.Precision.HIGHEST)
    trailing = reduced - jnp.dot(lower_part, upper_part, precision=lax.Precision.HIGHEST)
    row_global = lax.axis_index("prow") * piece_rows + jnp.arange(piece_rows)
    col_global = lax.axis_index("pcol") * piece_cols + jnp.arange(piece_cols)
    panel_cols = col_global < panel_width
    panel_rows = row_global < panel_width
    widened_lower = jnp.pad(lower_part, ((0, 0), (0, piece_cols - panel_width)))
    body_rows = jnp.where(panel_cols[None, :], widened_lower, trailing)
    head_rows = jnp.where(panel_cols[None, :], top_rows, upper_part)
    head_full = jnp.pad(head_rows, ((0, piece_rows - panel_width), (0, 0)))
    return jnp.where(panel_rows[:, None], head_full, body_rows)


def solution(mesh):
    in_specs = (
        P("prow", "pcol"),
        P(("layer", "prow", "pcol"), None, None),
        P(("layer", "prow", "pcol"), None, None),
        P(("layer", "prow", "pcol"), None),
        P(("layer", "prow", "pcol")),
        P(),
        P(),
    )
    return jax.shard_map(
        per_device, mesh=mesh, in_specs=in_specs, out_specs=P("prow", "pcol"), check_vma=False
    )
```

```python
import functools

import jax
import jax.numpy as jnp
from jax import lax
from jax.experimental import pallas as pl
from jax.experimental.pallas import tpu as pltpu
from jax.sharding import PartitionSpec as P

MESH = pl.DeviceIdType.MESH
GRID = 8
LAYERS = 4
OWNERS = GRID * GRID
BLOCK = 128
F32 = jnp.float32


def exchange_kernel(
    index_ref, table_ref, left_ref, right_ref, recv_ref, tables_ref, peak_ref,
    out_buf, table_buf, peak_buf, send_sem, recv_sem, own_sem, table_send, table_recv, peak_send, peak_recv,
):
    layer, row, col = lax.axis_index("layer"), lax.axis_index("prow"), lax.axis_index("pcol")
    me = row * GRID + col

    def place(k):
        r = (row + k % GRID) % GRID
        c = (col + k // GRID) % GRID
        return r, c

    def other(k):
        return ((layer + k) % LAYERS, row, col)

    barrier = pltpu.get_barrier_semaphore()

    def greet(k, carry):
        r, c = place(k)
        pl.semaphore_signal(barrier, inc=1, device_id=(layer, r, c), device_id_type=MESH)
        return carry

    lax.fori_loop(1, OWNERS, greet, 0)
    for k in range(1, LAYERS):
        pl.semaphore_signal(barrier, inc=1, device_id=other(k), device_id_type=MESH)

    def product(k):
        r, c = place(k)
        u = index_ref[r * GRID + c]
        out_buf[k] = jnp.dot(left_ref[u], right_ref[u], preferred_element_type=F32)

    def copy(k):
        r, c = place(k)
        return pltpu.make_async_remote_copy(
            src_ref=out_buf.at[k],
            dst_ref=recv_ref.at[me],
            send_sem=send_sem.at[k],
            recv_sem=recv_sem.at[k],
            device_id=(layer, r, c),
            device_id_type=MESH,
        )

    def table_copy(k):
        r, c = place(k)
        return pltpu.make_async_remote_copy(
            src_ref=table_ref,
            dst_ref=table_buf.at[me],
            send_sem=table_send.at[k],
            recv_sem=table_recv.at[k],
            device_id=(layer, r, c),
            device_id_type=MESH,
        )

    def peak_copy(k):
        return pltpu.make_async_remote_copy(
            src_ref=peak_buf.at[0],
            dst_ref=peak_buf.at[k],
            send_sem=peak_send.at[k],
            recv_sem=peak_recv.at[k],
            device_id=other(k),
            device_id_type=MESH,
        )

    product(0)
    product(1)
    pl.semaphore_wait(barrier, OWNERS - 1 + LAYERS - 1)

    def send_table(k, carry):
        table_copy(k).start()
        return carry

    def send(k, carry):
        copy(k).start()
        product(k + 1)
        return carry

    lax.fori_loop(1, OWNERS - 1, send, 0)
    copy(OWNERS - 1).start()
    lax.fori_loop(1, OWNERS, send_table, 0)
    own = pltpu.make_async_copy(out_buf.at[0], recv_ref.at[me], own_sem)
    own.start()
    table_buf[me] = table_ref[...]

    def finish_table(k, carry):
        table_copy(k).wait()
        return carry

    lax.fori_loop(1, OWNERS, finish_table, 0)
    tables_ref[...] = table_buf[...]
    peak_buf[0] = jnp.max(table_buf[...], axis=0)
    for k in range(1, LAYERS):
        peak_copy(k).start()
    own.wait()

    def finish(k, carry):
        copy(k).wait()
        return carry

    lax.fori_loop(1, OWNERS, finish, 0)
    for k in range(1, LAYERS):
        peak_copy(k).wait()
    peak_ref[...] = jnp.max(peak_buf[...], axis=0)


def exchange(index, table, left, right):
    vmem = pl.BlockSpec(memory_space=pltpu.VMEM)
    return pl.pallas_call(
        exchange_kernel,
        out_shape=(
            jax.ShapeDtypeStruct((OWNERS, BLOCK, BLOCK), F32),
            jax.ShapeDtypeStruct((OWNERS, 8, BLOCK), jnp.int32),
            jax.ShapeDtypeStruct((8, BLOCK), jnp.int32),
        ),
        in_specs=[pl.BlockSpec(memory_space=pltpu.SMEM), vmem, vmem, vmem],
        out_specs=(pl.BlockSpec(memory_space=pl.ANY), vmem, vmem),
        scratch_shapes=[
            pltpu.VMEM((OWNERS, BLOCK, BLOCK), F32),
            pltpu.VMEM((OWNERS, 8, BLOCK), jnp.int32),
            pltpu.VMEM((LAYERS, 8, BLOCK), jnp.int32),
            pltpu.SemaphoreType.DMA((OWNERS,)),
            pltpu.SemaphoreType.DMA((OWNERS,)),
            pltpu.SemaphoreType.DMA,
            pltpu.SemaphoreType.DMA((OWNERS,)),
            pltpu.SemaphoreType.DMA((OWNERS,)),
            pltpu.SemaphoreType.DMA((LAYERS,)),
            pltpu.SemaphoreType.DMA((LAYERS,)),
        ],
        compiler_params=pltpu.CompilerParams(
            collective_id=0, has_side_effects=True, vmem_limit_bytes=32 * 1024 * 1024
        ),
        cost_estimate=pl.CostEstimate(
            flops=2 * OWNERS * BLOCK**3, bytes_accessed=16 * 1024 * 1024, transcendentals=0
        ),
    )(index, table, left, right)


def scatter_kernel(per_step, spot_ref, extra_ref, recv_ref, extra_hbm, out_ref, extra_buf, extra_sem):
    step = pl.program_id(0)

    @pl.when(step == 0)
    def _():
        out_ref[...] = jnp.zeros_like(out_ref)

    def add(k, carry):
        spot = spot_ref[step * per_step + k]

        @pl.when(spot < 64)
        def _():
            out_ref[spot] += recv_ref[k]

        return carry

    lax.fori_loop(0, per_step, add, 0)

    def add_extra(k, carry):
        spot = extra_ref[step * per_step + k]

        @pl.when(spot < 64)
        def _():
            fetch = pltpu.make_async_copy(extra_hbm.at[step * per_step + k], extra_buf, extra_sem)
            fetch.start()
            fetch.wait()
            out_ref[spot] += extra_buf[...]

        return carry

    lax.fori_loop(0, per_step, add_extra, 0)


def scatter(spots, extra_spots, recv, extra):
    per_step = 8
    return pl.pallas_call(
        functools.partial(scatter_kernel, per_step),
        out_shape=jax.ShapeDtypeStruct((64, BLOCK, BLOCK), F32),
        grid=(OWNERS // per_step,),
        in_specs=[
            pl.BlockSpec(memory_space=pltpu.SMEM),
            pl.BlockSpec(memory_space=pltpu.SMEM),
            pl.BlockSpec((per_step, BLOCK, BLOCK), lambda i: (i, 0, 0)),
            pl.BlockSpec(memory_space=pl.ANY),
        ],
        out_specs=pl.BlockSpec((64, BLOCK, BLOCK), lambda i: (0, 0, 0)),
        scratch_shapes=[pltpu.VMEM((BLOCK, BLOCK), F32), pltpu.SemaphoreType.DMA],
        compiler_params=pltpu.CompilerParams(vmem_limit_bytes=24 * 1024 * 1024),
    )(spots, extra_spots, recv, extra)


def scatter_extra_kernel(extra_ref, dense_ref, extra_ref_data, out_ref):
    out_ref[...] = dense_ref[...]

    def add(k, carry):
        spot = extra_ref[k]

        @pl.when(spot < 64)
        def _():
            out_ref[spot] += extra_ref_data[k]

        return carry

    lax.fori_loop(0, OWNERS, add, 0)


def scatter_extra(extra_spots, dense, extra):
    return pl.pallas_call(
        scatter_extra_kernel,
        out_shape=jax.ShapeDtypeStruct((64, BLOCK, BLOCK), F32),
        in_specs=[
            pl.BlockSpec(memory_space=pltpu.SMEM),
            pl.BlockSpec(memory_space=pltpu.VMEM),
            pl.BlockSpec(memory_space=pltpu.VMEM),
        ],
        out_specs=pl.BlockSpec(memory_space=pltpu.VMEM),
        compiler_params=pltpu.CompilerParams(vmem_limit_bytes=24 * 1024 * 1024),
    )(extra_spots, dense, extra)


def local_sum(left, right, owners, spots):
    update_count = left.shape[0]
    most = update_count // 2
    destination = owners[:, 0]
    counter = jnp.arange(update_count)
    same = destination[:, None] == destination[None, :]
    rank = jnp.sum(same & (counter[None, :] < counter[:, None]), axis=1)
    named = (destination[None, :] == jnp.arange(OWNERS)[:, None]) & (rank == 0)[None, :]
    index = jnp.sum(jnp.where(named, counter[None, :], 0), axis=1)
    first_spot = jnp.sum(jnp.where(named, spots[None, :], 0), axis=1)
    first_spot = jnp.where(jnp.any(named, axis=1), first_spot, 64)
    second = rank == 1
    order = jnp.sum(second[None, :] & (counter[None, :] < counter[:, None]), axis=1)
    picked = second[None, :] & (order[None, :] == jnp.arange(most)[:, None])
    extra_index = jnp.sum(jnp.where(picked, counter[None, :], 0), axis=1)
    extra_code = jnp.sum(jnp.where(picked, destination[None, :] * 64 + spots[None, :], 0), axis=1)
    extra_code = jnp.where(jnp.any(picked, axis=1), extra_code, -1)
    count = jnp.sum(second).astype(jnp.int32)
    table = jnp.concatenate([first_spot, extra_code, jnp.full((32,), count)]).astype(jnp.int32)
    table = jnp.broadcast_to(table[None, :], (8, 128))
    col = lax.axis_index("pcol")
    me = lax.axis_index("prow") * GRID + col

    def slot_of(spot):
        i, j = spot // 8, spot % 8
        inside = jnp.where(j < 4, (i // 2) * 16 + j * 2 + i % 2, (2 * (j - 4) + 1) * 8 + i)
        return jnp.where(spot < 64, jnp.where(col == 0, inside, j * 8 + i), 64)

    def extra_round(k):
        u = extra_index[k]
        block = jnp.dot(left[u], right[u], preferred_element_type=F32)
        blocks = lax.all_gather(block[None], ("prow", "pcol"), axis=0, tiled=True)
        code = lax.dynamic_index_in_dim(layer_table, OWNERS + k, 1, keepdims=False)
        extra_spots = jnp.where((code >= 0) & (code // 64 == me), code % 64, 64)
        return slot_of(extra_spots), blocks

    recv, tables, peak = exchange(index, table, left, right)
    layer_table = tables[:, 0, :]
    rounds = peak[0, 96]
    my_spots = slot_of(lax.dynamic_index_in_dim(layer_table, me, 1, keepdims=False))
    extra_spots, blocks = extra_round(0)
    dense = scatter(my_spots, extra_spots, recv, blocks)

    def body(carry):
        k, dense = carry
        extra_spots, blocks = extra_round(k)
        return k + 1, scatter_extra(extra_spots, dense, blocks)

    return lax.while_loop(lambda carry: carry[0] < rounds, body, (jnp.int32(1), dense))[1]


def split(x):
    high = x.astype(jnp.bfloat16)
    return high, (x - high.astype(F32)).astype(jnp.bfloat16)


def dot(a, b):
    return jnp.dot(a, b, preferred_element_type=F32)


def panel_kernel(
    dense_ref, sep_ref, inv_ref, pivot_ref, out_ref,
    sep_buf, relay, comb, plain, red, top, left, low, up_hi, up_lo, up, perm, inv_lp, inv_u,
    sep_sem, rs_send, rs_recv, top_send, top_recv, ly_send, ly_recv, lx_send, lx_recv, lc_send, lc_recv,
    ag_send, ag_recv, fw_send, fw_recv, out_sem,
):
    layer, row, col = lax.axis_index("layer"), lax.axis_index("prow"), lax.axis_index("pcol")
    core = col % 2
    nxt, prv, opp = (layer + 1) % LAYERS, (layer + 3) % LAYERS, (layer + 2) % LAYERS
    edge = col == 0
    head = row == 0
    half = 4 * BLOCK

    def remote(src, dst, send, recv, device):
        return pltpu.make_async_remote_copy(
            src_ref=src, dst_ref=dst, send_sem=send, recv_sem=recv, device_id=device, device_id_type=MESH
        )

    to_nxt, to_prv, to_opp = (nxt, row, col), (prv, row, col), (opp, row, col)
    up_row, down_row = (row + 1) % GRID, (row + GRID - 1) % GRID

    barrier = pltpu.get_barrier_semaphore()
    for device in (to_nxt, to_prv, to_opp, (layer, up_row, col), (layer, down_row, col)):
        pl.semaphore_signal(barrier, inc=1, device_id=device, device_id_type=MESH)
    for k in range(1, GRID):
        pl.semaphore_signal(barrier, inc=1, device_id=(layer, row, (col + k) % GRID), device_id_type=MESH)

    def sep_first():
        return pltpu.make_async_copy(
            sep_ref.at[:, pl.ds(pl.multiple_of(layer * 2 * BLOCK, BLOCK), BLOCK)], sep_buf.at[0], sep_sem.at[0]
        )

    def sep_edge(j):
        return pltpu.make_async_copy(
            sep_ref.at[pl.ds(pl.multiple_of(layer * 256, 256), 256), pl.ds(j * BLOCK, BLOCK)],
            sep_buf.at[0, pl.ds(j * 256, 256)],
            sep_sem.at[2 + j],
        )

    def column(q, h):
        normal = 2 * q + h
        return pl.multiple_of(jnp.where(edge, 4 + q, normal) * BLOCK, BLOCK)

    sep_second = pltpu.make_async_copy(
        sep_ref.at[:, pl.ds(column(layer, 1), BLOCK)], sep_buf.at[1], sep_sem.at[1]
    )
    sep_second.start()

    @pl.when(jnp.logical_not(edge))
    def _():
        sep_first().start()

    @pl.when(edge)
    def _():
        for j in range(4):
            sep_edge(j).start()

    pl.semaphore_wait(barrier, 5 + GRID - 1)

    relay_out = [
        remote(dense_ref.at[2 * opp], relay.at[0], rs_send.at[0], rs_recv.at[0], to_nxt),
        remote(dense_ref.at[2 * opp + 1], relay.at[1], rs_send.at[1], rs_recv.at[1], to_prv),
    ]
    plain_out = [
        remote(dense_ref.at[2 * prv], plain.at[0], rs_send.at[2], rs_recv.at[2], to_prv),
        remote(dense_ref.at[2 * nxt + 1], plain.at[1], rs_send.at[3], rs_recv.at[3], to_nxt),
    ]
    comb_out = [
        remote(relay.at[0], comb.at[0], rs_send.at[4], rs_recv.at[4], to_nxt),
        remote(relay.at[1], comb.at[1], rs_send.at[5], rs_recv.at[5], to_prv),
    ]
    relay_out[0].start()
    relay_out[1].start()
    plain_out[1].start()
    plain_out[0].start()

    inv = inv_ref[...]
    rows_at = lax.broadcasted_iota(jnp.int32, (half, half), 0)
    cols_at = lax.broadcasted_iota(jnp.int32, (half, half), 1)
    inv_f = inv.astype(F32)
    lower_inverse = jnp.where(rows_at > cols_at, inv_f, jnp.where(rows_at == cols_at, 1.0, 0.0))
    inv_u[...] = jnp.where(rows_at <= cols_at, inv_f, 0.0).astype(jnp.bfloat16)
    perm[...] = jnp.where(pivot_ref[...] == cols_at, 1.0, 0.0).astype(jnp.bfloat16)
    inv_lp[...] = dot(lower_inverse.astype(jnp.bfloat16), perm[...]).astype(jnp.bfloat16)

    relay_out[0].wait_recv()
    relay[0] += dense_ref[2 * nxt]
    comb_out[0].start()
    relay_out[1].wait_recv()
    relay[1] += dense_ref[2 * prv + 1]
    comb_out[1].start()

    @pl.when(jnp.logical_not(edge))
    def _():
        sep_first().wait()

    @pl.when(edge)
    def _():
        for j in range(4):
            sep_edge(j).wait()

    sep_second.wait()
    for h in range(2):
        plain_out[h].wait_recv()
        red[h] = sep_buf[h] - (dense_ref[2 * layer + h] + plain[h])
    for h in range(2):
        comb_out[h].wait_recv()
        red[h] -= comb[h]

    def top_copy(h, s, d):
        part = top.at[h, pl.ds(s * 256, 256)]
        return remote(
            part, part, top_send.at[d, h, s], top_recv.at[h, s],
            (layer, (up_row if d == 0 else down_row), col),
        )

    def top_wait(h, s):
        top_copy(h, s, 0).wait_recv()

    onward = jnp.logical_and(row >= 1, row <= 3)
    backward = row >= 6

    def for_top(action):
        for h in (1, 0):
            for s in range(2):
                if h == 1:
                    action(h, s)
                else:
                    pl.when(jnp.logical_not(edge))(functools.partial(action, h, s))

    @pl.when(head)
    def _():
        top[0] = red[0, :half]
        top[1] = red[1, :half]

        def action(h, s):
            top_copy(h, s, 0).start()
            top_copy(h, s, 1).start()

        for_top(action)

    @pl.when(jnp.logical_and(edge, jnp.logical_not(head)))
    def _():
        top[0] = jnp.zeros((half, BLOCK), F32)

    def left_y(k):
        c = (col + k) % GRID
        part = left.at[layer, pl.ds((c % 2) * half, half)]
        return remote(part, part, ly_send.at[k], ly_recv, (layer, row, c))

    @pl.when(edge)
    def _():
        left[layer] = red[0]
        for k in (2, 3, 6, 7, 4, 5, 1):
            left_y(k).start()

    @pl.when(jnp.logical_not(edge))
    def _():
        mine = left.at[layer, pl.ds(core * half, half)]
        remote(mine, mine, ly_send.at[0], ly_recv, (layer, row, (col + 1) % GRID)).wait_recv()

    def left_x(k):
        part = left.at[layer, pl.ds(core * half, half)]
        return remote(part, part, lx_send.at[k], lx_recv.at[k], ((layer + k) % LAYERS, row, col))

    def left_x_wait(k):
        part = left.at[(layer + LAYERS - k) % LAYERS, pl.ds(core * half, half)]
        remote(part, part, lx_send.at[k], lx_recv.at[k], ((layer + k) % LAYERS, row, col)).wait_recv()

    sibling = (layer, row, col + 1 - 2 * core)

    def left_c(k):
        part = left.at[(layer + k) % LAYERS, pl.ds(core * half, half)]
        return remote(part, part, lc_send.at[k], lc_recv.at[k], sibling)

    def left_c_wait(k):
        part = left.at[(layer + k) % LAYERS, pl.ds((1 - core) * half, half)]
        remote(part, part, lc_send.at[k], lc_recv.at[k], sibling).wait_recv()

    for k in (1, 3, 2):
        left_x(k).start()

    @pl.when(col != 1)
    def _():
        left_c(0).start()

    @pl.when(jnp.logical_not(head))
    def _():
        def action(h, s):
            top_wait(h, s)

            @pl.when(onward)
            def _():
                top_copy(h, s, 0).start()

            @pl.when(backward)
            def _():
                top_copy(h, s, 1).start()

        for_top(action)

    for k in (1, 3, 2):
        left_x_wait(k)
        left_c(LAYERS - k).start()

    top_both = jnp.concatenate([top[0], top[1]], axis=1)
    top_hi, top_lo = split(top_both)
    up[...] = dot(inv_lp[...], top_hi) + dot(inv_lp[...], top_lo)
    hi, lo = split(up[...])
    up_hi[...] = hi
    up_lo[...] = lo

    @pl.when(jnp.logical_not(edge))
    def _():
        left_c_wait(0)

    for k in range(1, LAYERS):
        left_c_wait(k)

    def send_part(r, h, d):
        return remote(
            red.at[h, pl.ds(pl.multiple_of(r * 256, 256), 256)],
            out_ref.at[pl.ds(pl.multiple_of(r * 256, 256), 256), pl.ds(column(layer, h), BLOCK)],
            ag_send.at[d, h, r], ag_recv.at[d, h, r], (to_nxt if d == 0 else to_prv),
        )

    def wait_part(r, h, d):
        send_part(r, h, d).wait_recv()

    def forward_part(r, d):
        q = prv if d == 0 else nxt
        part = out_ref.at[pl.ds(pl.multiple_of(r * 256, 256), 256), pl.ds(column(q, d), BLOCK)]
        return remote(part, part, fw_send.at[d, r], fw_recv.at[d, r], (to_nxt if d == 0 else to_prv))

    def compute(r, carry):
        at = pl.ds(pl.multiple_of(r * 256, 256), 256)
        quarter = left[r]
        rows = jnp.concatenate([quarter[256 * j : 256 * (j + 1)] for j in range(4)], axis=1)
        rows_hi, rows_lo = split(rows)
        lower = dot(rows_hi, inv_u[...]) + dot(rows_lo, inv_u[...])
        low[at] = lower
        l_hi, l_lo = split(lower)
        u_hi, u_lo = up_hi[...], up_lo[...]
        change = dot(l_hi, u_hi) + (dot(l_lo, u_hi) + dot(l_hi, u_lo))
        in_head = jnp.logical_and(head, r < 2)
        upper = up[pl.ds(pl.multiple_of((r % 2) * 256, 256), 256)]
        for h in range(2):
            cut = slice(h * BLOCK, (h + 1) * BLOCK)
            red[h, at] = jnp.where(in_head, upper[:, cut], red[h, at] - change[:, cut])

        @pl.when(jnp.logical_not(edge))
        def _():
            send_part(r, 0, 0).start()
            send_part(r, 0, 1).start()

        send_part(r, 1, 1).start()
        send_part(r, 1, 0).start()
        return carry

    lax.fori_loop(0, LAYERS, compute, 0)

    def own_part(h):
        return pltpu.make_async_copy(red.at[h], out_ref.at[:, pl.ds(column(layer, h), BLOCK)], out_sem.at[h])

    own_part(1).start()

    @pl.when(jnp.logical_not(edge))
    def _():
        own_part(0).start()

    lower_copy = pltpu.make_async_copy(low, out_ref.at[:, pl.ds(0, half)], out_sem.at[2])

    @pl.when(edge)
    def _():
        @pl.when(head)
        def _():
            quarters = []
            for q in range(2):
                quarters.append(jnp.concatenate([left[q, 256 * j : 256 * (j + 1)] for j in range(4)], axis=1))
            rows = jnp.concatenate(quarters, axis=0)
            first, rest = split(rows)
            second, third = split(rows - first.astype(F32))
            low[:half] = dot(perm[...], first) + dot(perm[...], second) + dot(perm[...], third)

        lower_copy.start()

    def pass_on(r, carry):
        @pl.when(jnp.logical_not(edge))
        def _():
            wait_part(r, 0, 0)
            forward_part(r, 0).start()

        wait_part(r, 1, 1)
        forward_part(r, 1).start()
        return carry

    lax.fori_loop(0, LAYERS, pass_on, 0)

    def finish(r, carry):
        @pl.when(jnp.logical_not(edge))
        def _():
            wait_part(r, 0, 1)
            forward_wait(r, 0)
            send_part(r, 0, 0).wait_send()
            send_part(r, 0, 1).wait_send()
            forward_part(r, 0).wait_send()

        wait_part(r, 1, 0)
        forward_wait(r, 1)
        send_part(r, 1, 0).wait_send()
        send_part(r, 1, 1).wait_send()
        forward_part(r, 1).wait_send()
        return carry

    def forward_wait(r, d):
        forward_part(r, d).wait_recv()

    lax.fori_loop(0, LAYERS, finish, 0)

    for op in relay_out + plain_out + comb_out:
        op.wait_send()

    def sent(h, s):
        @pl.when(jnp.logical_or(head, onward))
        def _():
            top_copy(h, s, 0).wait_send()

        @pl.when(jnp.logical_or(head, backward))
        def _():
            top_copy(h, s, 1).wait_send()

    for_top(sent)

    @pl.when(edge)
    def _():
        for k in range(1, GRID):
            left_y(k).wait_send()

    for k in range(1, LAYERS):
        left_x(k).wait_send()
        left_c(k).wait_send()

    @pl.when(col != 1)
    def _():
        left_c(0).wait_send()

    own_part(1).wait()

    @pl.when(jnp.logical_not(edge))
    def _():
        own_part(0).wait()

    @pl.when(edge)
    def _():
        lower_copy.wait()


def panel(dense, separator, inverses, pivots):
    rows, cols = separator.shape
    half = 4 * BLOCK
    vmem = pl.BlockSpec(memory_space=pltpu.VMEM)
    hbm = pl.BlockSpec(memory_space=pl.ANY)
    dma = pltpu.SemaphoreType.DMA
    strip = (2, rows, BLOCK)
    bf16 = jnp.bfloat16
    return pl.pallas_call(
        panel_kernel,
        out_shape=jax.ShapeDtypeStruct((rows, cols), F32),
        in_specs=[vmem, hbm, vmem, vmem],
        out_specs=hbm,
        scratch_shapes=[
            pltpu.VMEM(strip, F32),
            pltpu.VMEM(strip, F32),
            pltpu.VMEM(strip, F32),
            pltpu.VMEM(strip, F32),
            pltpu.VMEM(strip, F32),
            pltpu.VMEM((2, half, BLOCK), F32),
            pltpu.VMEM((LAYERS, rows, BLOCK), F32),
            pltpu.VMEM((rows, half), F32),
            pltpu.VMEM((half, 256), bf16),
            pltpu.VMEM((half, 256), bf16),
            pltpu.VMEM((half, 256), F32),
            pltpu.VMEM((half, half), bf16),
            pltpu.VMEM((half, half), bf16),
            pltpu.VMEM((half, half), bf16),
            dma((6,)),
            dma((6,)),
            dma((6,)),
            dma((2, 2, 2)),
            dma((2, 2)),
            dma((GRID,)),
            dma,
            dma((LAYERS,)),
            dma((LAYERS,)),
            dma((LAYERS,)),
            dma((LAYERS,)),
            dma((2, 2, LAYERS)),
            dma((2, 2, LAYERS)),
            dma((2, LAYERS)),
            dma((2, LAYERS)),
            dma((3,)),
        ],
        compiler_params=pltpu.CompilerParams(
            collective_id=1, has_side_effects=True, vmem_limit_bytes=40 * 1024 * 1024
        ),
    )(dense, separator, inverses, pivots)


def per_device(separator, left_factor, right_factor, owners, spots, pivot_order, panel_inverses):
    dense = local_sum(left_factor, right_factor, owners, spots)
    return panel(dense.reshape(8, 1024, BLOCK), separator, panel_inverses, pivot_order[:, None])


def solution(mesh):
    in_specs = (
        P("prow", "pcol"),
        P(("layer", "prow", "pcol"), None, None),
        P(("layer", "prow", "pcol"), None, None),
        P(("layer", "prow", "pcol"), None),
        P(("layer", "prow", "pcol")),
        P(),
        P(),
    )
    return jax.shard_map(
        per_device, mesh=mesh, in_specs=in_specs, out_specs=P("prow", "pcol"), check_vma=False
    )
```

```python
import functools

import jax
import jax.numpy as jnp
from jax import lax
from jax.experimental import pallas as pl
from jax.experimental.pallas import tpu as pltpu
from jax.sharding import PartitionSpec as P

MESH = pl.DeviceIdType.MESH
GRID = 8
LAYERS = 4
OWNERS = GRID * GRID
BLOCK = 128
SLICES = 4
THIN = BLOCK // SLICES
F32 = jnp.float32
I32 = jnp.int32


def broadcast(x, axis, root):
    mine = lax.axis_index(axis) == root
    return lax.psum(jnp.where(mine, x, jnp.zeros_like(x)), axis)


def general(separator, left_factor, right_factor, owners, spots, pivot_order, panel_inverses):
    panel_width = pivot_order.shape[0]
    update_count = left_factor.shape[0]
    block_size = left_factor.shape[1]
    grid_rows = lax.axis_size("prow")
    grid_cols = lax.axis_size("pcol")
    owner_count = grid_rows * grid_cols
    capacity = 2 * update_count // owner_count
    slots_total = owner_count * capacity
    piece_rows, piece_cols = separator.shape
    per_row = piece_rows // block_size
    per_col = piece_cols // block_size
    square = block_size * block_size
    products = jnp.einsum(
        "uab,ubc->uac", left_factor, right_factor, preferred_element_type=jnp.float32
    )
    destination = owners[:, 0]
    chosen = (destination[:, None] == jnp.arange(owner_count)[None, :]).astype(jnp.float32)
    strict_lower = jnp.tril(jnp.ones((update_count, update_count), jnp.float32), -1)
    earlier = jnp.dot(strict_lower, chosen, precision=lax.Precision.HIGHEST)
    slot_rank = jnp.sum(earlier * chosen, axis=1).astype(jnp.int32)
    slot_index = destination * capacity + slot_rank
    dispatch = jnp.arange(slots_total)[:, None] == slot_index[None, :]
    outgoing = jnp.dot(
        dispatch.astype(jnp.float32),
        products.reshape(update_count, square),
        precision=lax.Precision.HIGHEST,
    )
    outgoing_spots = jnp.sum(jnp.where(dispatch, spots[None, :], 0), axis=1)
    arrived, arrived_spots = (
        lax.all_to_all(outgoing, ("prow", "pcol"), split_axis=0, concat_axis=0, tiled=True),
        lax.all_to_all(outgoing_spots, ("prow", "pcol"), split_axis=0, concat_axis=0, tiled=True),
    )
    placing = (arrived_spots[:, None] == jnp.arange(per_row * per_col)[None, :]).astype(jnp.float32)
    gathered = jnp.einsum("rp,rq->pq", placing, arrived, precision=lax.Precision.HIGHEST)
    local_sum = (
        gathered.reshape(per_row, per_col, block_size, block_size)
        .transpose(0, 2, 1, 3)
        .reshape(piece_rows, piece_cols)
    )
    reduced = separator - lax.psum(local_sum, "layer")
    top_rows = jnp.take(reduced[:panel_width], pivot_order, axis=0)
    left_block = reduced[:, :panel_width]
    inverses = panel_inverses.astype(jnp.float32)
    lower_inverse = jnp.tril(inverses, -1) + jnp.eye(panel_width, dtype=jnp.float32)
    upper_inverse = jnp.triu(inverses)
    upper_rows = broadcast(top_rows, "prow", 0)
    left_columns = broadcast(left_block, "pcol", 0)
    upper_part = jnp.dot(lower_inverse, upper_rows, precision=lax.Precision.HIGHEST)
    lower_part = jnp.dot(left_columns, upper_inverse, precision=lax.Precision.HIGHEST)
    trailing = reduced - jnp.dot(lower_part, upper_part, precision=lax.Precision.HIGHEST)
    row_global = lax.axis_index("prow") * piece_rows + jnp.arange(piece_rows)
    col_global = lax.axis_index("pcol") * piece_cols + jnp.arange(piece_cols)
    panel_cols = col_global < panel_width
    panel_rows = row_global < panel_width
    widened_lower = jnp.pad(lower_part, ((0, 0), (0, piece_cols - panel_width)))
    body_rows = jnp.where(panel_cols[None, :], widened_lower, trailing)
    head_rows = jnp.where(panel_cols[None, :], top_rows, upper_part)
    head_full = jnp.pad(head_rows, ((0, piece_rows - panel_width), (0, 0)))
    return jnp.where(panel_rows[:, None], head_full, body_rows)


def split(x):
    high = x.astype(jnp.bfloat16)
    return high, (x - high.astype(F32)).astype(jnp.bfloat16)


def dot(a, b):
    return jnp.dot(a, b, preferred_element_type=F32)


def turned(row):
    return jnp.broadcast_to(row, (BLOCK, BLOCK)).T


def fused_kernel(
    named_ref, left_ref, right_ref, sep_ref, inv_ref, pivot_ref, out_ref, peak_ref,
    main_0, main_1, main_2, main_3, extras, out_buf, table, table_buf, peak_buf, index_buf, index_mem, sorted_buf, sorted_mem, running, dense,
    sep_buf, relay, comb, plain, red, top, left, low, up_hi, up_lo, up, perm, inv_lp, inv_u,
    a_send, a_recv, t_send, t_recv, p_send, p_recv, z_send, z_recv, oy_send, oy_recv, oc_send, oc_recv, mem_sem,
    sep_sem, rs_send, rs_recv, top_send, top_recv, ly_send, ly_recv, lx_send, lx_recv, lc_send, lc_recv,
    ag_send, ag_recv, fw_send, fw_recv, out_sem,
):
    layer, row, col = lax.axis_index("layer"), lax.axis_index("prow"), lax.axis_index("pcol")
    me = row * GRID + col
    core = col % 2
    nxt, prv, opp = (layer + 1) % LAYERS, (layer + 3) % LAYERS, (layer + 2) % LAYERS
    edge = col == 0
    head = row == 0
    half = 4 * BLOCK
    mains = (main_0, main_1, main_2, main_3)

    def remote(src, dst, send, recv, device):
        return pltpu.make_async_remote_copy(
            src_ref=src, dst_ref=dst, send_sem=send, recv_sem=recv, device_id=device, device_id_type=MESH
        )

    to_nxt, to_prv, to_opp = (nxt, row, col), (prv, row, col), (opp, row, col)
    up_row, down_row = (row + 1) % GRID, (row + GRID - 1) % GRID
    sibling = (layer, row, col + 1 - 2 * core)

    def place(k):
        return (row + k % GRID) % GRID, (col + k // GRID) % GRID

    barrier = pltpu.get_barrier_semaphore()

    def greet(k, carry):
        r, c = place(k)
        pl.semaphore_signal(barrier, inc=1, device_id=(layer, r, c), device_id_type=MESH)
        return carry

    lax.fori_loop(1, OWNERS, greet, 0)
    for device in (to_nxt, to_prv, to_opp):
        pl.semaphore_signal(barrier, inc=1, device_id=device, device_id_type=MESH)

    def sep_first():
        return pltpu.make_async_copy(
            sep_ref.at[:, pl.ds(pl.multiple_of(layer * 2 * BLOCK, BLOCK), BLOCK)], sep_buf.at[0], sep_sem.at[0]
        )

    def sep_edge(j):
        return pltpu.make_async_copy(
            sep_ref.at[pl.ds(pl.multiple_of(layer * 256, 256), 256), pl.ds(j * BLOCK, BLOCK)],
            sep_buf.at[0, pl.ds(j * 256, 256)],
            sep_sem.at[2 + j],
        )

    def column(q, h):
        normal = 2 * q + h
        return pl.multiple_of(jnp.where(edge, 4 + q, normal) * BLOCK, BLOCK)

    sep_second = pltpu.make_async_copy(
        sep_ref.at[:, pl.ds(column(layer, 1), BLOCK)], sep_buf.at[1], sep_sem.at[1]
    )
    sep_second.start()

    @pl.when(jnp.logical_not(edge))
    def _():
        sep_first().start()

    @pl.when(edge)
    def _():
        for j in range(4):
            sep_edge(j).start()

    lane = lax.broadcasted_iota(I32, (OWNERS, BLOCK), 1)
    line = lax.broadcasted_iota(I32, (OWNERS, BLOCK), 0)
    named_row = jnp.broadcast_to(named_ref[...], (BLOCK, BLOCK))
    named_col = named_row.T
    owner_row, owner_col, spot_col = named_row[:OWNERS], named_col[:OWNERS], named_col[OWNERS:]

    def down(x):
        return jnp.sum(x, axis=0, keepdims=True)

    rank = jnp.sum(jnp.where((owner_row == owner_col) & (lane < line), 1, 0), axis=1, keepdims=True)
    rank = jnp.broadcast_to(rank, (OWNERS, BLOCK))
    hit = (owner_col == lane) & (rank == 0)
    index_row = down(jnp.where(hit, line, 0))
    spot_row = down(jnp.where(hit, spot_col, 0))
    hits = down(jnp.where(hit, 1, 0))
    second = rank == 1
    count_row = down(jnp.where(second, 1, 0))
    chosen = jnp.min(jnp.where(second, line, OWNERS), axis=0, keepdims=True)
    pick = line == chosen
    code_row = down(jnp.where(pick, owner_col * 64 + spot_col, 0))
    chosen_row = down(jnp.where(pick, line, 0))
    lane_row = lax.broadcasted_iota(I32, (1, BLOCK), 1)
    index_row = jnp.where(lane_row < OWNERS, index_row, chosen_row)
    spot_row = jnp.where(hits > 0, spot_row, 64)
    code_row = jnp.where(count_row > 0, code_row, -1)
    table_row = jnp.where(lane_row < OWNERS, spot_row, jnp.where(lane_row == OWNERS, code_row, count_row))
    table[...] = jnp.broadcast_to(table_row, (8, BLOCK))
    index_buf[...] = jnp.broadcast_to(index_row, (8, BLOCK))
    to_mem = pltpu.make_async_copy(index_buf, index_mem, mem_sem.at[0])
    to_mem.start()
    to_mem.wait()

    def multiply(u):
        return jnp.dot(left_ref[u], right_ref[u], preferred_element_type=F32)

    def product(k):
        r, c = place(k)
        out_buf[k] = multiply(index_mem[0, r * GRID + c])

    def slice_copy(k, s):
        r, c = place(k)
        rows = pl.ds(s * THIN, THIN)
        return remote(
            out_buf.at[k, rows], mains[s].at[row, col], a_send.at[s, k], a_recv.at[s, k], (layer, r, c)
        )

    def table_copy(k):
        r, c = place(k)
        return remote(table, table_buf.at[me], t_send.at[k], t_recv.at[k], (layer, r, c))

    def peak_copy(k):
        return remote(
            peak_buf.at[0], peak_buf.at[k], p_send.at[k], p_recv.at[k], ((layer + k) % LAYERS, row, col)
        )

    def ring_copy(d, h):
        source = (row + GRID - h + 1) % GRID if d == 0 else (row + h - 1) % GRID
        part = extras.at[source, col]
        return remote(part, part, z_send.at[d, h], z_recv.at[d, h], (layer, (up_row if d == 0 else down_row), col))

    def ring_start(h):
        ring_copy(0, h).start()
        if h <= 3:
            ring_copy(1, h).start()

    def ring_wait(h):
        ring_copy(0, h).wait_recv()
        if h <= 3:
            ring_copy(1, h).wait_recv()

    def across_copy(k):
        part = extras.at[:, col]
        return remote(part, part, oy_send.at[k], oy_recv.at[k], (layer, row, (col + 2 * k) % GRID))

    def core_copy(k):
        part = extras.at[:, (col + GRID - 2 * k) % GRID]
        return remote(part, part, oc_send.at[k], oc_recv.at[k], sibling)

    extras[row, col] = multiply(index_mem[0, OWNERS])
    product(1)
    product(2)
    pl.semaphore_wait(barrier, OWNERS - 1 + LAYERS - 1)
    ring_start(1)

    def first_slice(k, carry):
        slice_copy(k, 0).start()
        table_copy(k).start()
        product(k + 2)
        return carry

    def send_slice(s):
        def send(k, carry):
            slice_copy(k, s).start()
            return carry

        lax.fori_loop(1, OWNERS, send, 0)

    lax.fori_loop(1, 9, first_slice, 0)
    for h in range(1, 4):
        ring_wait(h)
        ring_start(h + 1)
        lax.fori_loop(1 + 8 * h, 9 + 8 * h, first_slice, 0)
    ring_wait(4)
    for k in (1, 3, 2):
        across_copy(k).start()
    core_copy(0).start()
    lax.fori_loop(33, OWNERS - 2, first_slice, 0)
    for k in (OWNERS - 2, OWNERS - 1):
        slice_copy(k, 0).start()
        table_copy(k).start()
    own = multiply(index_mem[0, me])
    for s in range(SLICES):
        mains[s][row, col] = own[s * THIN : (s + 1) * THIN]
    send_slice(1)

    inv = inv_ref[...]
    rows_at = lax.broadcasted_iota(jnp.int32, (half, half), 0)
    cols_at = lax.broadcasted_iota(jnp.int32, (half, half), 1)
    inv_f = inv.astype(F32)
    lower_inverse = jnp.where(rows_at > cols_at, inv_f, jnp.where(rows_at == cols_at, 1.0, 0.0))
    inv_u[...] = jnp.where(rows_at <= cols_at, inv_f, 0.0).astype(jnp.bfloat16)
    perm[...] = jnp.where(pivot_ref[...] == cols_at, 1.0, 0.0).astype(jnp.bfloat16)
    inv_lp[...] = dot(lower_inverse.astype(jnp.bfloat16), perm[...]).astype(jnp.bfloat16)

    table_buf[me] = table[...]

    def table_wait(k, carry):
        table_copy(k).wait()
        return carry

    lax.fori_loop(1, OWNERS, table_wait, 0)
    peak_buf[0] = jnp.max(table_buf[...], axis=0)
    for k in range(1, LAYERS):
        peak_copy(k).start()

    tables = table_buf[:, 0, :]
    mine = jnp.sum(jnp.where(lane == me, tables, 0), axis=1, keepdims=True)
    code = jnp.sum(jnp.where(lane == OWNERS, tables, 0), axis=1, keepdims=True)
    extra = jnp.where((code >= 0) & ((code >> 6) == me), code & 63, 64)
    spot = jnp.concatenate([mine, extra], axis=0)
    i, j = spot >> 3, spot & 7
    inside = jnp.where(j < 4, (i >> 1) * 16 + j * 2 + (i & 1), (2 * (j - 4) + 1) * 8 + i)
    slot = jnp.where(spot < 64, jnp.where(edge, inside, j * 8 + i), 64)
    slot_col = jnp.broadcast_to(slot, (BLOCK, BLOCK))
    slot_row = slot_col.T
    line2 = lax.broadcasted_iota(I32, (BLOCK, BLOCK), 0)
    lane2 = lax.broadcasted_iota(I32, (BLOCK, BLOCK), 1)
    ahead = (slot_row < slot_col) | ((slot_row == slot_col) & (lane2 < line2))
    rank2 = jnp.broadcast_to(jnp.sum(jnp.where(ahead, 1, 0), axis=1, keepdims=True), (BLOCK, BLOCK))
    order_row = down(jnp.where(rank2 == lane2, line2, 0))
    slots_row = down(jnp.where(rank2 == lane2, slot_col, 0))
    before_row = down(jnp.where(rank2 == lane2 - 1, slot_col, 0))
    same_row = jnp.where((slots_row == before_row) & (lane_row > 0), 1, 0)
    last_row = down(jnp.where(slot_col <= lane2, 1, 0)) - 1
    filled_row = jnp.where(down(jnp.where(slot_col == lane2, 1, 0)) > 0, 1, 0)
    last_row = jnp.maximum(last_row, 0)
    sorted_buf[0:1] = order_row
    sorted_buf[1:2] = same_row
    sorted_buf[2:3] = last_row
    sorted_buf[3:4] = filled_row
    sorted_buf[4:8] = jnp.zeros((4, BLOCK), I32)
    to_sorted = pltpu.make_async_copy(sorted_buf, sorted_mem, mem_sem.at[1])
    to_sorted.start()

    for k in (1, 3, 2):
        across_copy(k).wait_recv()
        core_copy(k).start()
    to_sorted.wait()
    for k in range(LAYERS):
        core_copy(k).wait_recv()

    def add_up(s):
        rows = pl.ds(s * THIN, THIN)

        def run(k, total):
            e = sorted_mem[0, k]
            near, far = jnp.minimum(e, OWNERS - 1), jnp.maximum(e - OWNERS, 0)
            value = jnp.where(
                e < OWNERS, mains[s][near >> 3, near & 7], extras[far >> 3, far & 7, rows, :]
            )
            total = value + jnp.where(sorted_mem[1, k] == 1, total, 0.0)
            running[k] = total
            return total

        lax.fori_loop(0, 2 * OWNERS, run, jnp.zeros((THIN, BLOCK), F32), unroll=8)

        def settle(k, carry):
            value = running[sorted_mem[2, k]]
            dense[s, k] = jnp.where(sorted_mem[3, k] == 1, value, 0.0)
            return carry

        lax.fori_loop(0, OWNERS, settle, 0, unroll=8)

    def strip(s, q):
        return dense.at[s, pl.ds(pl.multiple_of(8 * q, 8), 8)]

    def relay_out(s):
        return [
            remote(strip(s, 2 * opp), relay.at[0, s], rs_send.at[0, s], rs_recv.at[0, s], to_nxt),
            remote(strip(s, 2 * opp + 1), relay.at[1, s], rs_send.at[1, s], rs_recv.at[1, s], to_prv),
        ]

    def plain_out(s):
        return [
            remote(strip(s, 2 * prv), plain.at[0, s], rs_send.at[2, s], rs_recv.at[2, s], to_prv),
            remote(strip(s, 2 * nxt + 1), plain.at[1, s], rs_send.at[3, s], rs_recv.at[3, s], to_nxt),
        ]

    def comb_out(s):
        return [
            remote(relay.at[0, s], comb.at[0, s], rs_send.at[4, s], rs_recv.at[4, s], to_nxt),
            remote(relay.at[1, s], comb.at[1, s], rs_send.at[5, s], rs_recv.at[5, s], to_prv),
        ]

    def combine(s):
        relays, combs = relay_out(s), comb_out(s)
        for h, q in ((0, 2 * nxt), (1, 2 * prv + 1)):
            relays[h].wait_recv()
            relay[h, s] += dense[s, pl.ds(pl.multiple_of(8 * q, 8), 8)]
            combs[h].start()

    for s in range(SLICES):
        def slice_wait(k, carry):
            slice_copy(k, s).wait_recv()
            return carry

        lax.fori_loop(1, OWNERS, slice_wait, 0)
        add_up(s)
        for op in relay_out(s) + plain_out(s):
            op.start()
        if s + 2 < SLICES:
            send_slice(s + 2)
        if s >= 1:
            combine(s - 1)
    combine(SLICES - 1)

    @pl.when(jnp.logical_not(edge))
    def _():
        sep_first().wait()

    @pl.when(edge)
    def _():
        for j in range(4):
            sep_edge(j).wait()

    sep_second.wait()

    def reduced(s, carry):
        plains, combs = plain_out(s), comb_out(s)
        for h in range(2):
            plains[h].wait_recv()
            combs[h].wait_recv()
            for b in range(8):
                at = pl.ds(pl.multiple_of(b * BLOCK + s * THIN, THIN), THIN)
                red[h, at] = sep_buf[h, at] - (dense[s, 8 * (2 * layer + h) + b] + plain[h, s, b] + comb[h, s, b])
        return carry

    lax.fori_loop(0, SLICES, reduced, 0)

    def exchange_sent():
        def one(k, carry):
            for s in range(SLICES):
                slice_copy(k, s).wait_send()
            return carry

        lax.fori_loop(1, OWNERS, one, 0)
        for k in range(1, LAYERS):
            peak_copy(k).wait()
            across_copy(k).wait_send()
        for k in range(LAYERS):
            core_copy(k).wait_send()
        for h in range(1, 5):
            ring_copy(0, h).wait_send()
            if h <= 3:
                ring_copy(1, h).wait_send()
        peak_ref[...] = jnp.max(peak_buf[...], axis=0)

    def top_copy(h, s, d):
        part = top.at[h, pl.ds(s * 256, 256)]
        return remote(
            part, part, top_send.at[d, h, s], top_recv.at[h, s],
            (layer, (up_row if d == 0 else down_row), col),
        )

    def top_wait(h, s):
        top_copy(h, s, 0).wait_recv()

    onward = jnp.logical_and(row >= 1, row <= 3)
    backward = row >= 6

    def for_top(action):
        for h in (1, 0):
            for s in range(2):
                if h == 1:
                    action(h, s)
                else:
                    pl.when(jnp.logical_not(edge))(functools.partial(action, h, s))

    @pl.when(head)
    def _():
        top[0] = red[0, :half]
        top[1] = red[1, :half]

        def action(h, s):
            top_copy(h, s, 0).start()
            top_copy(h, s, 1).start()

        for_top(action)

    @pl.when(jnp.logical_and(edge, jnp.logical_not(head)))
    def _():
        top[0] = jnp.zeros((half, BLOCK), F32)

    def left_y(k):
        c = (col + k) % GRID
        part = left.at[layer, pl.ds((c % 2) * half, half)]
        return remote(part, part, ly_send.at[k], ly_recv, (layer, row, c))

    @pl.when(edge)
    def _():
        left[layer] = red[0]
        for k in (2, 3, 6, 7, 4, 5, 1):
            left_y(k).start()

    @pl.when(jnp.logical_not(edge))
    def _():
        mine = left.at[layer, pl.ds(core * half, half)]
        remote(mine, mine, ly_send.at[0], ly_recv, (layer, row, (col + 1) % GRID)).wait_recv()

    def left_x(k):
        part = left.at[layer, pl.ds(core * half, half)]
        return remote(part, part, lx_send.at[k], lx_recv.at[k], ((layer + k) % LAYERS, row, col))

    def left_x_wait(k):
        part = left.at[(layer + LAYERS - k) % LAYERS, pl.ds(core * half, half)]
        remote(part, part, lx_send.at[k], lx_recv.at[k], ((layer + k) % LAYERS, row, col)).wait_recv()

    sibling = (layer, row, col + 1 - 2 * core)

    def left_c(k):
        part = left.at[(layer + k) % LAYERS, pl.ds(core * half, half)]
        return remote(part, part, lc_send.at[k], lc_recv.at[k], sibling)

    def left_c_wait(k):
        part = left.at[(layer + k) % LAYERS, pl.ds((1 - core) * half, half)]
        remote(part, part, lc_send.at[k], lc_recv.at[k], sibling).wait_recv()

    for k in (1, 3, 2):
        left_x(k).start()

    @pl.when(col != 1)
    def _():
        left_c(0).start()

    @pl.when(jnp.logical_not(head))
    def _():
        def action(h, s):
            top_wait(h, s)

            @pl.when(onward)
            def _():
                top_copy(h, s, 0).start()

            @pl.when(backward)
            def _():
                top_copy(h, s, 1).start()

        for_top(action)

    for k in (1, 3, 2):
        left_x_wait(k)
        left_c(LAYERS - k).start()

    top_both = jnp.concatenate([top[0], top[1]], axis=1)
    top_hi, top_lo = split(top_both)
    up[...] = dot(inv_lp[...], top_hi) + dot(inv_lp[...], top_lo)
    hi, lo = split(up[...])
    up_hi[...] = hi
    up_lo[...] = lo

    @pl.when(jnp.logical_not(edge))
    def _():
        left_c_wait(0)

    for k in range(1, LAYERS):
        left_c_wait(k)

    def send_part(r, h, d):
        return remote(
            red.at[h, pl.ds(pl.multiple_of(r * 256, 256), 256)],
            out_ref.at[pl.ds(pl.multiple_of(r * 256, 256), 256), pl.ds(column(layer, h), BLOCK)],
            ag_send.at[d, h, r], ag_recv.at[d, h, r], (to_nxt if d == 0 else to_prv),
        )

    def wait_part(r, h, d):
        send_part(r, h, d).wait_recv()

    def forward_part(r, d):
        q = prv if d == 0 else nxt
        part = out_ref.at[pl.ds(pl.multiple_of(r * 256, 256), 256), pl.ds(column(q, d), BLOCK)]
        return remote(part, part, fw_send.at[d, r], fw_recv.at[d, r], (to_nxt if d == 0 else to_prv))

    def compute(r, carry):
        at = pl.ds(pl.multiple_of(r * 256, 256), 256)
        quarter = left[r]
        rows = jnp.concatenate([quarter[256 * j : 256 * (j + 1)] for j in range(4)], axis=1)
        rows_hi, rows_lo = split(rows)
        lower = dot(rows_hi, inv_u[...]) + dot(rows_lo, inv_u[...])
        low[at] = lower
        l_hi, l_lo = split(lower)
        u_hi, u_lo = up_hi[...], up_lo[...]
        change = dot(l_hi, u_hi) + (dot(l_lo, u_hi) + dot(l_hi, u_lo))
        in_head = jnp.logical_and(head, r < 2)
        upper = up[pl.ds(pl.multiple_of((r % 2) * 256, 256), 256)]
        for h in range(2):
            cut = slice(h * BLOCK, (h + 1) * BLOCK)
            red[h, at] = jnp.where(in_head, upper[:, cut], red[h, at] - change[:, cut])

        @pl.when(jnp.logical_not(edge))
        def _():
            send_part(r, 0, 0).start()
            send_part(r, 0, 1).start()

        send_part(r, 1, 1).start()
        send_part(r, 1, 0).start()
        return carry

    lax.fori_loop(0, LAYERS, compute, 0)

    def own_part(h):
        return pltpu.make_async_copy(red.at[h], out_ref.at[:, pl.ds(column(layer, h), BLOCK)], out_sem.at[h])

    own_part(1).start()

    @pl.when(jnp.logical_not(edge))
    def _():
        own_part(0).start()

    lower_copy = pltpu.make_async_copy(low, out_ref.at[:, pl.ds(0, half)], out_sem.at[2])

    @pl.when(edge)
    def _():
        @pl.when(head)
        def _():
            quarters = []
            for q in range(2):
                quarters.append(jnp.concatenate([left[q, 256 * j : 256 * (j + 1)] for j in range(4)], axis=1))
            rows = jnp.concatenate(quarters, axis=0)
            first, rest = split(rows)
            second, third = split(rows - first.astype(F32))
            low[:half] = dot(perm[...], first) + dot(perm[...], second) + dot(perm[...], third)

        lower_copy.start()

    def pass_on(r, carry):
        @pl.when(jnp.logical_not(edge))
        def _():
            wait_part(r, 0, 0)
            forward_part(r, 0).start()

        wait_part(r, 1, 1)
        forward_part(r, 1).start()
        return carry

    lax.fori_loop(0, LAYERS, pass_on, 0)

    def finish(r, carry):
        @pl.when(jnp.logical_not(edge))
        def _():
            wait_part(r, 0, 1)
            forward_wait(r, 0)
            send_part(r, 0, 0).wait_send()
            send_part(r, 0, 1).wait_send()
            forward_part(r, 0).wait_send()

        wait_part(r, 1, 0)
        forward_wait(r, 1)
        send_part(r, 1, 0).wait_send()
        send_part(r, 1, 1).wait_send()
        forward_part(r, 1).wait_send()
        return carry

    def forward_wait(r, d):
        forward_part(r, d).wait_recv()

    lax.fori_loop(0, LAYERS, finish, 0)

    def sum_sent(s, carry):
        for op in relay_out(s) + plain_out(s) + comb_out(s):
            op.wait_send()
        return carry

    lax.fori_loop(0, SLICES, sum_sent, 0)
    exchange_sent()

    def sent(h, s):
        @pl.when(jnp.logical_or(head, onward))
        def _():
            top_copy(h, s, 0).wait_send()

        @pl.when(jnp.logical_or(head, backward))
        def _():
            top_copy(h, s, 1).wait_send()

    for_top(sent)

    @pl.when(edge)
    def _():
        for k in range(1, GRID):
            left_y(k).wait_send()

    for k in range(1, LAYERS):
        left_x(k).wait_send()
        left_c(k).wait_send()

    @pl.when(col != 1)
    def _():
        left_c(0).wait_send()

    own_part(1).wait()

    @pl.when(jnp.logical_not(edge))
    def _():
        own_part(0).wait()

    @pl.when(edge)
    def _():
        lower_copy.wait()


def fused(named, left, right, separator, inverses, pivots):
    rows, cols = separator.shape
    half = 4 * BLOCK
    vmem = pl.BlockSpec(memory_space=pltpu.VMEM)
    hbm = pl.BlockSpec(memory_space=pl.ANY)
    dma = pltpu.SemaphoreType.DMA
    strip = (2, rows, BLOCK)
    thin = (2, SLICES, 8, THIN, BLOCK)
    bf16 = jnp.bfloat16
    return pl.pallas_call(
        fused_kernel,
        out_shape=(jax.ShapeDtypeStruct((rows, cols), F32), jax.ShapeDtypeStruct((8, BLOCK), I32)),
        in_specs=[vmem, vmem, vmem, hbm, vmem, vmem],
        out_specs=(hbm, vmem),
        scratch_shapes=[
            pltpu.VMEM((GRID, GRID, THIN, BLOCK), F32),
            pltpu.VMEM((GRID, GRID, THIN, BLOCK), F32),
            pltpu.VMEM((GRID, GRID, THIN, BLOCK), F32),
            pltpu.VMEM((GRID, GRID, THIN, BLOCK), F32),
            pltpu.VMEM((GRID, GRID, BLOCK, BLOCK), F32),
            pltpu.VMEM((OWNERS, BLOCK, BLOCK), F32),
            pltpu.VMEM((8, BLOCK), I32),
            pltpu.VMEM((OWNERS, 8, BLOCK), I32),
            pltpu.VMEM((LAYERS, 8, BLOCK), I32),
            pltpu.VMEM((8, BLOCK), I32),
            pltpu.SMEM((8, BLOCK), I32),
            pltpu.VMEM((8, BLOCK), I32),
            pltpu.SMEM((8, BLOCK), I32),
            pltpu.VMEM((2 * OWNERS, THIN, BLOCK), F32),
            pltpu.VMEM((SLICES, OWNERS, THIN, BLOCK), F32),
            pltpu.VMEM(strip, F32),
            pltpu.VMEM(thin, F32),
            pltpu.VMEM(thin, F32),
            pltpu.VMEM(thin, F32),
            pltpu.VMEM(strip, F32),
            pltpu.VMEM((2, half, BLOCK), F32),
            pltpu.VMEM((LAYERS, rows, BLOCK), F32),
            pltpu.VMEM((rows, half), F32),
            pltpu.VMEM((half, 256), bf16),
            pltpu.VMEM((half, 256), bf16),
            pltpu.VMEM((half, 256), F32),
            pltpu.VMEM((half, half), bf16),
            pltpu.VMEM((half, half), bf16),
            pltpu.VMEM((half, half), bf16),
            dma((SLICES, OWNERS)),
            dma((SLICES, OWNERS)),
            dma((OWNERS,)),
            dma((OWNERS,)),
            dma((LAYERS,)),
            dma((LAYERS,)),
            dma((2, 5)),
            dma((2, 5)),
            dma((LAYERS,)),
            dma((LAYERS,)),
            dma((LAYERS,)),
            dma((LAYERS,)),
            dma((2,)),
            dma((6,)),
            dma((6, SLICES)),
            dma((6, SLICES)),
            dma((2, 2, 2)),
            dma((2, 2)),
            dma((GRID,)),
            dma,
            dma((LAYERS,)),
            dma((LAYERS,)),
            dma((LAYERS,)),
            dma((LAYERS,)),
            dma((2, 2, LAYERS)),
            dma((2, 2, LAYERS)),
            dma((2, LAYERS)),
            dma((2, LAYERS)),
            dma((3,)),
        ],
        compiler_params=pltpu.CompilerParams(
            collective_id=0, has_side_effects=True, vmem_limit_bytes=56 * 1024 * 1024
        ),
    )(named, left, right, separator, inverses, pivots)


def per_device(separator, left_factor, right_factor, owners, spots, pivot_order, panel_inverses):
    named = jnp.concatenate([owners[:, 0], spots])[None, :]
    result, peak = fused(named, left_factor, right_factor, separator, panel_inverses, pivot_order[:, None])
    return lax.cond(
        peak[0, BLOCK - 1] > 1,
        lambda: general(separator, left_factor, right_factor, owners, spots, pivot_order, panel_inverses),
        lambda: result,
    )


def solution(mesh):
    in_specs = (
        P("prow", "pcol"),
        P(("layer", "prow", "pcol"), None, None),
        P(("layer", "prow", "pcol"), None, None),
        P(("layer", "prow", "pcol"), None),
        P(("layer", "prow", "pcol")),
        P(),
        P(),
    )
    return jax.shard_map(
        per_device, mesh=mesh, in_specs=in_specs, out_specs=P("prow", "pcol"), check_vma=False
    )
```

```python
import functools

import jax
import jax.numpy as jnp
from jax import lax
from jax.experimental import pallas as pl
from jax.experimental.pallas import tpu as pltpu
from jax.sharding import PartitionSpec as P

MESH = pl.DeviceIdType.MESH
GRID = 8
LAYERS = 4
OWNERS = GRID * GRID
BLOCK = 128
THINS = (32, 32, 32, 32)
STARTS = tuple(sum(THINS[:s]) for s in range(len(THINS)))
SLICES = len(THINS)
AHEAD = 2
EARLY = 16
F32 = jnp.float32
BF16 = jnp.bfloat16
I32 = jnp.int32


def split(x):
    high = x.astype(BF16)
    return high, (x - high.astype(F32)).astype(BF16)


def dot(a, b):
    return jnp.dot(a, b, preferred_element_type=F32)


def down(x):
    return jnp.sum(x, axis=0, keepdims=True)


def across(x):
    return jnp.sum(x, axis=1, keepdims=True)


def wide(x):
    return jnp.broadcast_to(x, (x.shape[0], BLOCK))


def exchange_kernel(
    index_ref, table_ref, left_ref, right_ref, recv_ref, tables_ref,
    out_buf, table_buf, send_sem, recv_sem, own_sem, table_send, table_recv,
):
    layer, row, col = lax.axis_index("layer"), lax.axis_index("prow"), lax.axis_index("pcol")
    me = row * GRID + col

    def place(k):
        return (row + k % GRID) % GRID, (col + k // GRID) % GRID

    barrier = pltpu.get_barrier_semaphore()

    def greet(k, carry):
        r, c = place(k)
        pl.semaphore_signal(barrier, inc=1, device_id=(layer, r, c), device_id_type=MESH)
        return carry

    lax.fori_loop(1, OWNERS, greet, 0)

    def product(k):
        r, c = place(k)
        for t in range(2):
            u = index_ref[t * OWNERS + r * GRID + c]
            out_buf[k, t] = jnp.dot(left_ref[u], right_ref[u], preferred_element_type=F32)

    def copy(k):
        r, c = place(k)
        return pltpu.make_async_remote_copy(
            src_ref=out_buf.at[k],
            dst_ref=recv_ref.at[me],
            send_sem=send_sem.at[k],
            recv_sem=recv_sem.at[k],
            device_id=(layer, r, c),
            device_id_type=MESH,
        )

    def table_copy(k):
        r, c = place(k)
        return pltpu.make_async_remote_copy(
            src_ref=table_ref,
            dst_ref=table_buf.at[me],
            send_sem=table_send.at[k],
            recv_sem=table_recv.at[k],
            device_id=(layer, r, c),
            device_id_type=MESH,
        )

    pl.semaphore_wait(barrier, OWNERS - 1)

    def send(k, carry):
        product(k)
        copy(k).start()
        table_copy(k).start()
        return carry

    lax.fori_loop(1, OWNERS, send, 0)
    product(0)
    own = pltpu.make_async_copy(out_buf.at[0], recv_ref.at[me], own_sem)
    own.start()
    table_buf[me] = table_ref[...]

    def finish(k, carry):
        table_copy(k).wait()
        copy(k).wait()
        return carry

    lax.fori_loop(1, OWNERS, finish, 0)
    own.wait()
    tables_ref[...] = table_buf[...]


def exchange(index, table, left, right):
    vmem = pl.BlockSpec(memory_space=pltpu.VMEM)
    dma = pltpu.SemaphoreType.DMA
    return pl.pallas_call(
        exchange_kernel,
        out_shape=(
            jax.ShapeDtypeStruct((OWNERS, 2, BLOCK, BLOCK), F32),
            jax.ShapeDtypeStruct((OWNERS, 8, BLOCK), I32),
        ),
        in_specs=[pl.BlockSpec(memory_space=pltpu.SMEM), vmem, vmem, vmem],
        out_specs=(pl.BlockSpec(memory_space=pl.ANY), vmem),
        scratch_shapes=[
            pltpu.VMEM((OWNERS, 2, BLOCK, BLOCK), F32),
            pltpu.VMEM((OWNERS, 8, BLOCK), I32),
            dma((OWNERS,)),
            dma((OWNERS,)),
            dma,
            dma((OWNERS,)),
            dma((OWNERS,)),
        ],
        compiler_params=pltpu.CompilerParams(
            collective_id=1, has_side_effects=True, vmem_limit_bytes=32 * 1024 * 1024
        ),
    )(index, table, left, right)


def scatter_kernel(slot_ref, recv_ref, out_ref):
    step = pl.program_id(0)

    @pl.when(step == 0)
    def _():
        out_ref[...] = jnp.zeros_like(out_ref)

    def add(k, carry):
        slot = slot_ref[step * 8 + k]

        @pl.when(slot < 64)
        def _():
            out_ref[slot] += recv_ref[k]

        return carry

    lax.fori_loop(0, 8, add, 0)


def scatter(slots, recv):
    return pl.pallas_call(
        scatter_kernel,
        out_shape=jax.ShapeDtypeStruct((64, BLOCK, BLOCK), F32),
        grid=(2 * OWNERS // 8,),
        in_specs=[
            pl.BlockSpec(memory_space=pltpu.SMEM),
            pl.BlockSpec((8, BLOCK, BLOCK), lambda i: (i, 0, 0)),
        ],
        out_specs=pl.BlockSpec((64, BLOCK, BLOCK), lambda i: (0, 0, 0)),
        compiler_params=pltpu.CompilerParams(vmem_limit_bytes=24 * 1024 * 1024),
    )(slots, recv)


def panel_kernel(
    dense_ref, sep_ref, inv_ref, pivot_ref, out_ref,
    sep_buf, relay, comb, plain, red, top, left, low, up_hi, up_lo, up, perm, inv_lp, inv_u,
    sep_sem, rs_send, rs_recv, top_send, top_recv, ly_send, ly_recv, lx_send, lx_recv, lc_send, lc_recv,
    ag_send, ag_recv, fw_send, fw_recv, out_sem,
):
    layer, row, col = lax.axis_index("layer"), lax.axis_index("prow"), lax.axis_index("pcol")
    core = col % 2
    nxt, prv, opp = (layer + 1) % LAYERS, (layer + 3) % LAYERS, (layer + 2) % LAYERS
    edge = col == 0
    head = row == 0
    half = 4 * BLOCK

    def remote(src, dst, send, recv, device):
        return pltpu.make_async_remote_copy(
            src_ref=src, dst_ref=dst, send_sem=send, recv_sem=recv, device_id=device, device_id_type=MESH
        )

    to_nxt, to_prv, to_opp = (nxt, row, col), (prv, row, col), (opp, row, col)
    up_row, down_row = (row + 1) % GRID, (row + GRID - 1) % GRID

    barrier = pltpu.get_barrier_semaphore()
    for device in (to_nxt, to_prv, to_opp, (layer, up_row, col), (layer, down_row, col)):
        pl.semaphore_signal(barrier, inc=1, device_id=device, device_id_type=MESH)
    for k in range(1, GRID):
        pl.semaphore_signal(barrier, inc=1, device_id=(layer, row, (col + k) % GRID), device_id_type=MESH)

    def sep_first():
        return pltpu.make_async_copy(
            sep_ref.at[:, pl.ds(pl.multiple_of(layer * 2 * BLOCK, BLOCK), BLOCK)], sep_buf.at[0], sep_sem.at[0]
        )

    def sep_edge(j):
        return pltpu.make_async_copy(
            sep_ref.at[pl.ds(pl.multiple_of(layer * 256, 256), 256), pl.ds(j * BLOCK, BLOCK)],
            sep_buf.at[0, pl.ds(j * 256, 256)],
            sep_sem.at[2 + j],
        )

    def column(q, h):
        normal = 2 * q + h
        return pl.multiple_of(jnp.where(edge, 4 + q, normal) * BLOCK, BLOCK)

    sep_second = pltpu.make_async_copy(
        sep_ref.at[:, pl.ds(column(layer, 1), BLOCK)], sep_buf.at[1], sep_sem.at[1]
    )
    sep_second.start()

    @pl.when(jnp.logical_not(edge))
    def _():
        sep_first().start()

    @pl.when(edge)
    def _():
        for j in range(4):
            sep_edge(j).start()

    pl.semaphore_wait(barrier, 5 + GRID - 1)

    relay_out = [
        remote(dense_ref.at[2 * opp], relay.at[0], rs_send.at[0], rs_recv.at[0], to_nxt),
        remote(dense_ref.at[2 * opp + 1], relay.at[1], rs_send.at[1], rs_recv.at[1], to_prv),
    ]
    plain_out = [
        remote(dense_ref.at[2 * prv], plain.at[0], rs_send.at[2], rs_recv.at[2], to_prv),
        remote(dense_ref.at[2 * nxt + 1], plain.at[1], rs_send.at[3], rs_recv.at[3], to_nxt),
    ]
    comb_out = [
        remote(relay.at[0], comb.at[0], rs_send.at[4], rs_recv.at[4], to_nxt),
        remote(relay.at[1], comb.at[1], rs_send.at[5], rs_recv.at[5], to_prv),
    ]
    relay_out[0].start()
    relay_out[1].start()
    plain_out[1].start()
    plain_out[0].start()

    inv = inv_ref[...]
    rows_at = lax.broadcasted_iota(jnp.int32, (half, half), 0)
    cols_at = lax.broadcasted_iota(jnp.int32, (half, half), 1)
    inv_f = inv.astype(F32)
    lower_inverse = jnp.where(rows_at > cols_at, inv_f, jnp.where(rows_at == cols_at, 1.0, 0.0))
    inv_u[...] = jnp.where(rows_at <= cols_at, inv_f, 0.0).astype(jnp.bfloat16)
    perm[...] = jnp.where(pivot_ref[...] == cols_at, 1.0, 0.0).astype(jnp.bfloat16)
    inv_lp[...] = dot(lower_inverse.astype(jnp.bfloat16), perm[...]).astype(jnp.bfloat16)

    relay_out[0].wait_recv()
    relay[0] += dense_ref[2 * nxt]
    comb_out[0].start()
    relay_out[1].wait_recv()
    relay[1] += dense_ref[2 * prv + 1]
    comb_out[1].start()

    @pl.when(jnp.logical_not(edge))
    def _():
        sep_first().wait()

    @pl.when(edge)
    def _():
        for j in range(4):
            sep_edge(j).wait()

    sep_second.wait()
    for h in range(2):
        plain_out[h].wait_recv()
        red[h] = sep_buf[h] - (dense_ref[2 * layer + h] + plain[h])
    for h in range(2):
        comb_out[h].wait_recv()
        red[h] -= comb[h]

    def top_copy(h, s, d):
        part = top.at[h, pl.ds(s * 256, 256)]
        return remote(
            part, part, top_send.at[d, h, s], top_recv.at[h, s],
            (layer, (up_row if d == 0 else down_row), col),
        )

    def top_wait(h, s):
        top_copy(h, s, 0).wait_recv()

    onward = jnp.logical_and(row >= 1, row <= 3)
    backward = row >= 6

    def for_top(action):
        for h in (1, 0):
            for s in range(2):
                if h == 1:
                    action(h, s)
                else:
                    pl.when(jnp.logical_not(edge))(functools.partial(action, h, s))

    @pl.when(head)
    def _():
        top[0] = red[0, :half]
        top[1] = red[1, :half]

        def action(h, s):
            top_copy(h, s, 0).start()
            top_copy(h, s, 1).start()

        for_top(action)

    @pl.when(jnp.logical_and(edge, jnp.logical_not(head)))
    def _():
        top[0] = jnp.zeros((half, BLOCK), F32)

    def left_y(k):
        c = (col + k) % GRID
        part = left.at[layer, pl.ds((c % 2) * half, half)]
        return remote(part, part, ly_send.at[k], ly_recv, (layer, row, c))

    @pl.when(edge)
    def _():
        left[layer] = red[0]
        for k in (2, 3, 6, 7, 4, 5, 1):
            left_y(k).start()

    @pl.when(jnp.logical_not(edge))
    def _():
        mine = left.at[layer, pl.ds(core * half, half)]
        remote(mine, mine, ly_send.at[0], ly_recv, (layer, row, (col + 1) % GRID)).wait_recv()

    def left_x(k):
        part = left.at[layer, pl.ds(core * half, half)]
        return remote(part, part, lx_send.at[k], lx_recv.at[k], ((layer + k) % LAYERS, row, col))

    def left_x_wait(k):
        part = left.at[(layer + LAYERS - k) % LAYERS, pl.ds(core * half, half)]
        remote(part, part, lx_send.at[k], lx_recv.at[k], ((layer + k) % LAYERS, row, col)).wait_recv()

    sibling = (layer, row, col + 1 - 2 * core)

    def left_c(k):
        part = left.at[(layer + k) % LAYERS, pl.ds(core * half, half)]
        return remote(part, part, lc_send.at[k], lc_recv.at[k], sibling)

    def left_c_wait(k):
        part = left.at[(layer + k) % LAYERS, pl.ds((1 - core) * half, half)]
        remote(part, part, lc_send.at[k], lc_recv.at[k], sibling).wait_recv()

    for k in (1, 3, 2):
        left_x(k).start()

    @pl.when(col != 1)
    def _():
        left_c(0).start()

    @pl.when(jnp.logical_not(head))
    def _():
        def action(h, s):
            top_wait(h, s)

            @pl.when(onward)
            def _():
                top_copy(h, s, 0).start()

            @pl.when(backward)
            def _():
                top_copy(h, s, 1).start()

        for_top(action)

    for k in (1, 3, 2):
        left_x_wait(k)
        left_c(LAYERS - k).start()

    top_both = jnp.concatenate([top[0], top[1]], axis=1)
    top_hi, top_lo = split(top_both)
    up[...] = dot(inv_lp[...], top_hi) + dot(inv_lp[...], top_lo)
    hi, lo = split(up[...])
    up_hi[...] = hi
    up_lo[...] = lo

    @pl.when(jnp.logical_not(edge))
    def _():
        left_c_wait(0)

    for k in range(1, LAYERS):
        left_c_wait(k)

    def send_part(r, h, d):
        return remote(
            red.at[h, pl.ds(pl.multiple_of(r * 256, 256), 256)],
            out_ref.at[pl.ds(pl.multiple_of(r * 256, 256), 256), pl.ds(column(layer, h), BLOCK)],
            ag_send.at[d, h, r], ag_recv.at[d, h, r], (to_nxt if d == 0 else to_prv),
        )

    def wait_part(r, h, d):
        send_part(r, h, d).wait_recv()

    def forward_part(r, d):
        q = prv if d == 0 else nxt
        part = out_ref.at[pl.ds(pl.multiple_of(r * 256, 256), 256), pl.ds(column(q, d), BLOCK)]
        return remote(part, part, fw_send.at[d, r], fw_recv.at[d, r], (to_nxt if d == 0 else to_prv))

    def compute(r, carry):
        at = pl.ds(pl.multiple_of(r * 256, 256), 256)
        quarter = left[r]
        rows = jnp.concatenate([quarter[256 * j : 256 * (j + 1)] for j in range(4)], axis=1)
        rows_hi, rows_lo = split(rows)
        lower = dot(rows_hi, inv_u[...]) + dot(rows_lo, inv_u[...])
        low[at] = lower
        l_hi, l_lo = split(lower)
        u_hi, u_lo = up_hi[...], up_lo[...]
        change = dot(l_hi, u_hi) + (dot(l_lo, u_hi) + dot(l_hi, u_lo))
        in_head = jnp.logical_and(head, r < 2)
        upper = up[pl.ds(pl.multiple_of((r % 2) * 256, 256), 256)]
        for h in range(2):
            cut = slice(h * BLOCK, (h + 1) * BLOCK)
            red[h, at] = jnp.where(in_head, upper[:, cut], red[h, at] - change[:, cut])

        @pl.when(jnp.logical_not(edge))
        def _():
            send_part(r, 0, 0).start()
            send_part(r, 0, 1).start()

        send_part(r, 1, 1).start()
        send_part(r, 1, 0).start()
        return carry

    lax.fori_loop(0, LAYERS, compute, 0)

    def own_part(h):
        return pltpu.make_async_copy(red.at[h], out_ref.at[:, pl.ds(column(layer, h), BLOCK)], out_sem.at[h])

    own_part(1).start()

    @pl.when(jnp.logical_not(edge))
    def _():
        own_part(0).start()

    lower_copy = pltpu.make_async_copy(low, out_ref.at[:, pl.ds(0, half)], out_sem.at[2])

    @pl.when(edge)
    def _():
        @pl.when(head)
        def _():
            quarters = []
            for q in range(2):
                quarters.append(jnp.concatenate([left[q, 256 * j : 256 * (j + 1)] for j in range(4)], axis=1))
            rows = jnp.concatenate(quarters, axis=0)
            first, rest = split(rows)
            second, third = split(rows - first.astype(F32))
            low[:half] = dot(perm[...], first) + dot(perm[...], second) + dot(perm[...], third)

        lower_copy.start()

    def pass_on(r, carry):
        @pl.when(jnp.logical_not(edge))
        def _():
            wait_part(r, 0, 0)
            forward_part(r, 0).start()

        wait_part(r, 1, 1)
        forward_part(r, 1).start()
        return carry

    lax.fori_loop(0, LAYERS, pass_on, 0)

    def finish(r, carry):
        @pl.when(jnp.logical_not(edge))
        def _():
            wait_part(r, 0, 1)
            forward_wait(r, 0)
            send_part(r, 0, 0).wait_send()
            send_part(r, 0, 1).wait_send()
            forward_part(r, 0).wait_send()

        wait_part(r, 1, 0)
        forward_wait(r, 1)
        send_part(r, 1, 0).wait_send()
        send_part(r, 1, 1).wait_send()
        forward_part(r, 1).wait_send()
        return carry

    def forward_wait(r, d):
        forward_part(r, d).wait_recv()

    lax.fori_loop(0, LAYERS, finish, 0)

    for op in relay_out + plain_out + comb_out:
        op.wait_send()

    def sent(h, s):
        @pl.when(jnp.logical_or(head, onward))
        def _():
            top_copy(h, s, 0).wait_send()

        @pl.when(jnp.logical_or(head, backward))
        def _():
            top_copy(h, s, 1).wait_send()

    for_top(sent)

    @pl.when(edge)
    def _():
        for k in range(1, GRID):
            left_y(k).wait_send()

    for k in range(1, LAYERS):
        left_x(k).wait_send()
        left_c(k).wait_send()

    @pl.when(col != 1)
    def _():
        left_c(0).wait_send()

    own_part(1).wait()

    @pl.when(jnp.logical_not(edge))
    def _():
        own_part(0).wait()

    @pl.when(edge)
    def _():
        lower_copy.wait()


def panel(dense, separator, inverses, pivots):
    rows, cols = separator.shape
    half = 4 * BLOCK
    vmem = pl.BlockSpec(memory_space=pltpu.VMEM)
    hbm = pl.BlockSpec(memory_space=pl.ANY)
    dma = pltpu.SemaphoreType.DMA
    strip = (2, rows, BLOCK)
    bf16 = jnp.bfloat16
    return pl.pallas_call(
        panel_kernel,
        out_shape=jax.ShapeDtypeStruct((rows, cols), F32),
        in_specs=[vmem, hbm, vmem, vmem],
        out_specs=hbm,
        scratch_shapes=[
            pltpu.VMEM(strip, F32),
            pltpu.VMEM(strip, F32),
            pltpu.VMEM(strip, F32),
            pltpu.VMEM(strip, F32),
            pltpu.VMEM(strip, F32),
            pltpu.VMEM((2, half, BLOCK), F32),
            pltpu.VMEM((LAYERS, rows, BLOCK), F32),
            pltpu.VMEM((rows, half), F32),
            pltpu.VMEM((half, 256), bf16),
            pltpu.VMEM((half, 256), bf16),
            pltpu.VMEM((half, 256), F32),
            pltpu.VMEM((half, half), bf16),
            pltpu.VMEM((half, half), bf16),
            pltpu.VMEM((half, half), bf16),
            dma((6,)),
            dma((6,)),
            dma((6,)),
            dma((2, 2, 2)),
            dma((2, 2)),
            dma((GRID,)),
            dma,
            dma((LAYERS,)),
            dma((LAYERS,)),
            dma((LAYERS,)),
            dma((LAYERS,)),
            dma((2, 2, LAYERS)),
            dma((2, 2, LAYERS)),
            dma((2, LAYERS)),
            dma((2, LAYERS)),
            dma((3,)),
        ],
        compiler_params=pltpu.CompilerParams(
            collective_id=2, has_side_effects=True, vmem_limit_bytes=40 * 1024 * 1024
        ),
    )(dense, separator, inverses, pivots)


def general(separator, left_factor, right_factor, owners, spots, pivot_order, panel_inverses):
    destination = owners[:, 0]
    counter = jnp.arange(OWNERS)
    same = destination[:, None] == destination[None, :]
    rank = jnp.sum(same & (counter[None, :] < counter[:, None]), axis=1)
    named = (destination[None, :] == jnp.arange(2 * OWNERS)[:, None] % OWNERS) & (
        rank[None, :] == jnp.arange(2 * OWNERS)[:, None] // OWNERS
    )
    index = jnp.sum(jnp.where(named, counter[None, :], 0), axis=1).astype(I32)
    placed = jnp.where(jnp.any(named, axis=1), jnp.sum(jnp.where(named, spots[None, :], 0), axis=1), 64)
    table = jnp.broadcast_to(placed.astype(I32)[None, :], (8, 2 * OWNERS))
    recv, tables = exchange(index, table, left_factor, right_factor)
    col = lax.axis_index("pcol")
    me = lax.axis_index("prow") * GRID + col
    arrived = lax.dynamic_index_in_dim(tables[:, 0, :].reshape(OWNERS, 2, OWNERS), me, 2, keepdims=False)
    spot = arrived.reshape(2 * OWNERS)
    i, j = spot // 8, spot % 8
    inside = jnp.where(j < 4, (i // 2) * 16 + j * 2 + i % 2, (2 * (j - 4) + 1) * 8 + i)
    slots = jnp.where(spot < 64, jnp.where(col == 0, inside, j * 8 + i), 64)
    dense = scatter(slots, recv.reshape(2 * OWNERS, BLOCK, BLOCK))
    return panel(dense.reshape(8, 1024, BLOCK), separator, panel_inverses, pivot_order[:, None])


SCRATCH = (
    ("mains", "each", lambda n: ((2 * GRID, GRID, n, BLOCK), F32)),
    ("dense", "each", lambda n: ((OWNERS, n, BLOCK), F32)),
    ("relay", "each", lambda n: ((2, 8, n, BLOCK), F32)),
    ("comb", "each", lambda n: ((2, 8, n, BLOCK), F32)),
    ("plain", "each", lambda n: ((2, 8, n, BLOCK), F32)),
    ("piece", "each", lambda n: ((8, 8, n, BLOCK), F32)),
    ("top", "each", lambda n: ((8, 4, n, BLOCK), F32)),
    ("left", "each", lambda n: ((LAYERS, 8, n, BLOCK), F32)),
    ("low", "each", lambda n: ((8 * n, 512), F32)),
    ("low_hi", "each", lambda n: ((8 * n, 512), BF16)),
    ("low_lo", "each", lambda n: ((8 * n, 512), BF16)),
    ("result", "each", lambda n: ((8, n, 1024), F32)),
    ("ring", "one", ((GRID, BLOCK, BLOCK), F32)),
    ("out_buf", "one", ((OWNERS, BLOCK, BLOCK), F32)),
    ("table_buf", "one", ((GRID, GRID, 8, BLOCK), I32)),
    ("peak_buf", "one", ((LAYERS, 8, BLOCK), I32)),
    ("index_buf", "one", ((8, BLOCK), I32)),
    ("sorted_buf", "one", ((8, BLOCK), I32)),
    ("running", "one", ((2 * OWNERS, max(THINS), BLOCK), F32)),
    ("sep_buf", "one", ((2, 1024, BLOCK), F32)),
    ("up", "one", ((512, 1024), F32)),
    ("up_hi", "one", ((512, 1024), BF16)),
    ("up_lo", "one", ((512, 1024), BF16)),
    ("inv_lp", "one", ((512, 512), BF16)),
    ("inv_u", "one", ((512, 512), BF16)),
    ("perm", "one", ((512, 512), BF16)),
    ("index_mem", "smem", ((8, BLOCK), I32)),
    ("sorted_mem", "smem", ((8, BLOCK), I32)),
    ("a_sem", "sem", (2, SLICES, OWNERS)),
    ("p_sem", "sem", (2, LAYERS)),
    ("z_sem", "sem", (2, 2, 2, 5)),
    ("y_sem", "sem", (2, SLICES, LAYERS)),
    ("c_sem", "sem", (2, SLICES, LAYERS)),
    ("ty_sem", "sem", (2, LAYERS)),
    ("tc_sem", "sem", (2, LAYERS)),
    ("mem_sem", "sem", (2,)),
    ("sep_sem", "sem", (6,)),
    ("rs_sem", "sem", (2, SLICES, 6)),
    ("ag_sem", "sem", (2, SLICES, 2, 2)),
    ("fw_sem", "sem", (2, SLICES, 2)),
    ("top_sem", "sem", (3, SLICES, 2)),
    ("tx_sem", "sem", (2, SLICES, 2, LAYERS)),
    ("ly_sem", "sem", (SLICES, 1 + GRID)),
    ("lx_sem", "sem", (2, SLICES, LAYERS)),
    ("lc_sem", "sem", (2, SLICES, LAYERS)),
    ("out_sem", "sem", (SLICES, 8)),
)


def scratch_shapes():
    shapes = []
    for _, kind, what in SCRATCH:
        if kind == "each":
            shapes += [pltpu.VMEM(*what(n)) for n in THINS]
        elif kind == "one":
            shapes.append(pltpu.VMEM(*what))
        elif kind == "smem":
            shapes.append(pltpu.SMEM(*what))
        else:
            shapes.append(pltpu.SemaphoreType.DMA(what))
    return shapes


class Scratch:
    def __init__(self, refs):
        at = 0
        for name, kind, _ in SCRATCH:
            if kind == "each":
                setattr(self, name, refs[at : at + SLICES])
                at += SLICES
            else:
                setattr(self, name, refs[at])
                at += 1


def fused_kernel(
    owners_ref, spots_ref, left_ref, right_ref, sep_ref, inv_ref, pivot_ref, out_ref, peak_ref, *refs
):
    b = Scratch(refs)
    layer, row, col = lax.axis_index("layer"), lax.axis_index("prow"), lax.axis_index("pcol")
    me = row * GRID + col
    core = col % 2
    nxt, prv, opp = (layer + 1) % LAYERS, (layer + 3) % LAYERS, (layer + 2) % LAYERS
    edge = col == 0
    inner = jnp.logical_not(edge)
    head = row == 0
    up_row, down_row = (row + 1) % GRID, (row + GRID - 1) % GRID
    to_nxt, to_prv = (nxt, row, col), (prv, row, col)
    sibling = (layer, row, col + 1 - 2 * core)

    def remote(src, dst, sems, device):
        return pltpu.make_async_remote_copy(
            src_ref=src, dst_ref=dst, send_sem=sems[0], recv_sem=sems[1], device_id=device, device_id_type=MESH
        )

    def pair(sem, *at):
        return sem.at[(0, *at)], sem.at[(1, *at)]

    def place(k):
        return (row + k % GRID) % GRID, (col + k // GRID) % GRID

    def other(k):
        return ((layer + k) % LAYERS, row, col)

    def column(q, h):
        return jnp.where(edge, 4 + q, 2 * q + h)

    barrier = pltpu.get_barrier_semaphore()

    def greet(k, carry):
        r, c = place(k)
        pl.semaphore_signal(barrier, inc=1, device_id=(layer, r, c), device_id_type=MESH)
        return carry

    lax.fori_loop(1, OWNERS, greet, 0)
    for k in range(1, LAYERS):
        pl.semaphore_signal(barrier, inc=1, device_id=other(k), device_id_type=MESH)

    def sep_whole(h):
        return pltpu.make_async_copy(
            sep_ref.at[:, pl.ds(pl.multiple_of(column(layer, h) * BLOCK, BLOCK), BLOCK)],
            b.sep_buf.at[h],
            b.sep_sem.at[h],
        )

    def sep_edge(j):
        return pltpu.make_async_copy(
            sep_ref.at[pl.ds(pl.multiple_of(layer * 256, 256), 256), pl.ds(j * BLOCK, BLOCK)],
            b.sep_buf.at[0, pl.ds(j * 256, 256)],
            b.sep_sem.at[2 + j],
        )

    sep_whole(1).start()

    @pl.when(inner)
    def _():
        sep_whole(0).start()

    @pl.when(edge)
    def _():
        for j in range(4):
            sep_edge(j).start()

    lane = lax.broadcasted_iota(I32, (OWNERS, BLOCK), 1)
    line = lax.broadcasted_iota(I32, (OWNERS, BLOCK), 0)
    lane_row = lax.broadcasted_iota(I32, (1, BLOCK), 1)
    owner_all = jnp.broadcast_to(jnp.concatenate([owners_ref[...], spots_ref[...]], axis=1), (BLOCK, BLOCK))
    owner_row, both = owner_all[:OWNERS], owner_all.T
    owner_col, spot_col = both[:OWNERS], both[OWNERS:]
    rank = wide(across(jnp.where((owner_row == owner_col) & (lane < line), 1, 0)))
    hit = (owner_col == lane) & (rank == 0)
    index_row = down(jnp.where(hit, line, 0))
    spot_row = down(jnp.where(hit, spot_col, 0))
    hits = down(jnp.where(hit, 1, 0))
    second = rank == 1
    count_row = down(jnp.where(second, 1, 0))
    chosen = jnp.min(jnp.where(second, line, OWNERS), axis=0, keepdims=True)
    pick = line == chosen
    code_row = down(jnp.where(pick, owner_col * 64 + spot_col, 0))
    chosen_row = down(jnp.where(pick, line, 0))
    index_row = jnp.where(lane_row < OWNERS, index_row, chosen_row)
    spot_row = jnp.where(hits > 0, spot_row, 64)
    code_row = jnp.where(count_row > 0, code_row, -1)
    table_row = jnp.where(lane_row < OWNERS, spot_row, jnp.where(lane_row == OWNERS, code_row, count_row))
    b.table_buf[row, col] = jnp.broadcast_to(table_row, (8, BLOCK))
    b.index_buf[...] = jnp.broadcast_to(index_row, (8, BLOCK))
    to_mem = pltpu.make_async_copy(b.index_buf, b.index_mem, b.mem_sem.at[0])
    to_mem.start()
    to_mem.wait()

    def multiply(u):
        return dot(left_ref[u], right_ref[u])

    def product(k):
        r, c = place(k)
        b.out_buf[k] = multiply(b.index_mem[0, r * GRID + c])

    def slice_copy(k, s):
        r, c = place(k)
        return remote(
            b.out_buf.at[k, pl.ds(STARTS[s], THINS[s])], b.mains[s].at[row, col], pair(b.a_sem, s, k), (layer, r, c)
        )

    def peak_copy(k):
        return remote(b.peak_buf.at[0], b.peak_buf.at[k], pair(b.p_sem, k), other(k))

    def ring_copies(h):
        copies = []
        for d in range(2 if h <= 3 else 1):
            source = (row + GRID - h + 1) % GRID if d == 0 else (row + h - 1) % GRID
            device = (layer, (up_row if d == 0 else down_row), col)
            block, table = b.ring.at[source], b.table_buf.at[source, col]
            copies.append(remote(block, block, pair(b.z_sem, 0, d, h), device))
            copies.append(remote(table, table, pair(b.z_sem, 1, d, h), device))
        return copies

    def row_copy(s, k):
        return remote(
            b.ring.at[:, pl.ds(STARTS[s], THINS[s])],
            b.mains[s].at[pl.ds(GRID, GRID), col],
            pair(b.y_sem, s, k),
            (layer, row, (col + 2 * k) % GRID),
        )

    def core_copy(s, k):
        part = b.mains[s].at[pl.ds(GRID, GRID), (col + GRID - 2 * k) % GRID]
        return remote(part, part, pair(b.c_sem, s, k), sibling)

    def row_table(k):
        part = b.table_buf.at[:, col]
        return remote(part, part, pair(b.ty_sem, k), (layer, row, (col + 2 * k) % GRID))

    def core_table(k):
        part = b.table_buf.at[:, (col + GRID - 2 * k) % GRID]
        return remote(part, part, pair(b.tc_sem, k), sibling)

    def early(k, carry):
        product(k)
        return carry

    b.ring[row] = multiply(b.index_mem[0, OWNERS])
    lax.fori_loop(1, 1 + EARLY, early, 0, unroll=4)
    pl.semaphore_wait(barrier, OWNERS - 1 + LAYERS - 1)

    def first_slice(k, carry):
        slice_copy(k, 0).start()
        product(k + EARLY)
        return carry

    def send_slice(s, first=1):
        def send(k, carry):
            slice_copy(k, s).start()
            return carry

        lax.fori_loop(first, OWNERS, send, 0)

    for op in ring_copies(1):
        op.start()
    lax.fori_loop(1, 9, first_slice, 0)
    for h in range(1, 4):
        for op in ring_copies(h):
            op.wait_recv()
        for op in ring_copies(h + 1):
            op.start()
        lax.fori_loop(1 + 8 * h, 9 + 8 * h, first_slice, 0)
    for op in ring_copies(4):
        op.wait_recv()
    for k in (1, 3, 2):
        row_table(k).start()
    core_table(0).start()
    for s in range(SLICES):
        for k in (1, 3, 2):
            row_copy(s, k).start()
        for r in range(GRID):
            b.mains[s][GRID + r, col] = b.ring[r, pl.ds(STARTS[s], THINS[s])]
        core_copy(s, 0).start()
    lax.fori_loop(33, OWNERS - EARLY, first_slice, 0)
    send_slice(0, OWNERS - EARLY)
    own = multiply(b.index_mem[0, me])
    for s in range(SLICES):
        b.mains[s][row, col] = own[STARTS[s] : STARTS[s] + THINS[s]]
    for s in range(1, AHEAD):
        send_slice(s)

    inv = inv_ref[...].astype(F32)
    rows_at = lax.broadcasted_iota(I32, (512, 512), 0)
    cols_at = lax.broadcasted_iota(I32, (512, 512), 1)
    lower_inverse = jnp.where(rows_at > cols_at, inv, jnp.where(rows_at == cols_at, 1.0, 0.0)).astype(BF16)
    b.inv_u[...] = jnp.where(rows_at <= cols_at, inv, 0.0).astype(BF16)
    for s in range(SLICES):
        n = 4 * THINS[s]
        at = lax.broadcasted_iota(I32, (n, 512), 0)
        source = (at // THINS[s]) * BLOCK + STARTS[s] + at % THINS[s]
        b.perm[pl.ds(4 * STARTS[s], n)] = jnp.where(pivot_ref[...] == source, 1.0, 0.0).astype(BF16)
    b.inv_lp[...] = lax.dot_general(
        lower_inverse, b.perm[...], (((1,), (1,)), ((), ())), preferred_element_type=F32
    ).astype(BF16)

    for k in (1, 3, 2):
        row_table(k).wait_recv()
        core_table(k).start()
    for k in range(LAYERS):
        core_table(k).wait_recv()
    tables = b.table_buf[...].reshape(OWNERS, 8, BLOCK)
    b.peak_buf[0] = jnp.max(tables, axis=0)
    for k in range(1, LAYERS):
        peak_copy(k).start()
    tables = tables[:, 0, :]
    mine = across(jnp.where(lane == me, tables, 0))
    code = across(jnp.where(lane == OWNERS, tables, 0))
    extra = jnp.where((code >= 0) & ((code >> 6) == me), code & 63, 64)
    spot = jnp.concatenate([mine, extra], axis=0)
    i, j = spot >> 3, spot & 7
    inside = jnp.where(j < 4, (i >> 1) * 16 + j * 2 + (i & 1), (2 * (j - 4) + 1) * 8 + i)
    slot_col = wide(jnp.where(spot < 64, jnp.where(edge, inside, j * 8 + i), 64))
    slot_row = slot_col.T
    line2 = lax.broadcasted_iota(I32, (BLOCK, BLOCK), 0)
    lane2 = lax.broadcasted_iota(I32, (BLOCK, BLOCK), 1)
    ahead = (slot_row < slot_col) | ((slot_row == slot_col) & (lane2 < line2))
    rank2 = wide(across(jnp.where(ahead, 1, 0)))
    order_row = down(jnp.where(rank2 == lane2, line2, 0))
    slots_row = down(jnp.where(rank2 == lane2, slot_col, 0))
    before_row = down(jnp.where(rank2 == lane2 - 1, slot_col, 0))
    same_row = jnp.where((slots_row == before_row) & (lane_row > 0), 1, 0)
    last_row = jnp.maximum(down(jnp.where(slot_col <= lane2, 1, 0)) - 1, 0)
    filled_row = jnp.where(down(jnp.where(slot_col == lane2, 1, 0)) > 0, 1, 0)
    b.sorted_buf[0:1] = order_row
    b.sorted_buf[1:2] = same_row
    b.sorted_buf[2:3] = last_row
    b.sorted_buf[3:4] = filled_row
    b.sorted_buf[4:8] = jnp.zeros((4, BLOCK), I32)
    to_sorted = pltpu.make_async_copy(b.sorted_buf, b.sorted_mem, b.mem_sem.at[1])
    to_sorted.start()
    to_sorted.wait()

    def spread_extras(s):
        for k in (1, 3, 2):
            row_copy(s, k).wait_recv()
            core_copy(s, k).start()

    def add_up(s):
        thin = pl.ds(0, THINS[s])

        def run(k, total):
            e = b.sorted_mem[0, k]
            total = b.mains[s][e >> 3, e & 7] + jnp.where(b.sorted_mem[1, k] == 1, total, 0.0)
            b.running[k, thin] = total
            return total

        lax.fori_loop(0, 2 * OWNERS, run, jnp.zeros((THINS[s], BLOCK), F32), unroll=8)

        def settle(k, carry):
            value = b.running[b.sorted_mem[2, k], thin]
            b.dense[s][k] = jnp.where(b.sorted_mem[3, k] == 1, value, 0.0)
            return carry

        lax.fori_loop(0, OWNERS, settle, 0, unroll=8)

    def strip(s, q):
        return b.dense[s].at[pl.ds(pl.multiple_of(8 * q, 8), 8)]

    def relay_out(s):
        return [
            remote(strip(s, 2 * opp), b.relay[s].at[0], pair(b.rs_sem, s, 0), to_nxt),
            remote(strip(s, 2 * opp + 1), b.relay[s].at[1], pair(b.rs_sem, s, 1), to_prv),
        ]

    def plain_out(s):
        return [
            remote(strip(s, 2 * prv), b.plain[s].at[0], pair(b.rs_sem, s, 2), to_prv),
            remote(strip(s, 2 * nxt + 1), b.plain[s].at[1], pair(b.rs_sem, s, 3), to_nxt),
        ]

    def comb_out(s):
        return [
            remote(b.relay[s].at[0], b.comb[s].at[0], pair(b.rs_sem, s, 4), to_nxt),
            remote(b.relay[s].at[1], b.comb[s].at[1], pair(b.rs_sem, s, 5), to_prv),
        ]

    def combine(s):
        relays, combs = relay_out(s), comb_out(s)
        for h, q in ((0, 2 * nxt), (1, 2 * prv + 1)):
            relays[h].wait_recv()
            b.relay[s][h] += b.dense[s][pl.ds(pl.multiple_of(8 * q, 8), 8)]
            combs[h].start()

    def gather_copy(s, h, d):
        part = b.piece[s].at[column(layer, h)]
        return remote(part, part, pair(b.ag_sem, s, h, d), to_nxt if d == 0 else to_prv)

    def gather_pass(s, d):
        part = b.piece[s].at[column(prv if d == 0 else nxt, d)]
        return remote(part, part, pair(b.fw_sem, s, d), to_nxt if d == 0 else to_prv)

    def top_copy(s, h, d):
        part = b.top[s].at[column(layer, h)]
        device = (layer, up_row if d == 0 else down_row, col)
        return remote(part, part, (b.top_sem.at[d, s, h], b.top_sem.at[2, s, h]), device)

    def top_other(s, h, k):
        part = b.top[s].at[column(layer, h)]
        return remote(part, part, pair(b.tx_sem, s, h, k), other(k))

    onward = jnp.logical_and(row >= 1, row <= 3)
    backward = row >= 6

    def left_part(s, q, c):
        return b.left[s].at[q, pl.ds(pl.multiple_of((c % 2) * 4, 4), 4)]

    def left_row(s, k):
        c = (col + k) % GRID
        part = left_part(s, layer, c)
        return remote(part, part, (b.ly_sem.at[s, k], b.ly_sem.at[s, 0]), (layer, row, c))

    def left_row_wait(s):
        part = left_part(s, layer, col)
        op = remote(part, part, (b.ly_sem.at[s, 1], b.ly_sem.at[s, 0]), (layer, row, (col + 1) % GRID))
        op.wait_recv()

    def left_other(s, k):
        part = left_part(s, layer, col)
        return remote(part, part, pair(b.lx_sem, s, k), other(k))

    def left_core(s, k):
        part = left_part(s, (layer + k) % LAYERS, col)
        return remote(part, part, pair(b.lc_sem, s, k), sibling)

    def halves(action):
        action(1)
        pl.when(inner)(lambda: action(0))

    def reduce(s):
        plains, combs = plain_out(s), comb_out(s)
        n = THINS[s]

        def value(h, k):
            return b.sep_buf[h, pl.ds(k * BLOCK + STARTS[s], n)] - (
                b.dense[s][8 * (2 * layer + h) + k] + b.plain[s][h, k] + b.comb[s][h, k]
            )

        for h in range(2):
            plains[h].wait_recv()
            combs[h].wait_recv()
        for k in range(8):
            b.piece[s][column(layer, 1), k] = value(1, k)

        @pl.when(inner)
        def _():
            for k in range(8):
                b.piece[s][2 * layer, k] = value(0, k)

        @pl.when(edge)
        def _():
            for k in range(8):
                b.left[s][layer, k] = value(0, k)
            for k in (2, 6, 3, 7, 4, 5, 1):
                left_row(s, k).start()

        @pl.when(head)
        def _():
            def keep(h):
                b.top[s][column(layer, h)] = b.piece[s][column(layer, h), pl.ds(0, 4)]

            halves(keep)

        @pl.when(inner)
        def _():
            gather_copy(s, 0, 0).start()
            gather_copy(s, 0, 1).start()

        gather_copy(s, 1, 1).start()
        gather_copy(s, 1, 0).start()

    def top_out(s):
        @pl.when(head)
        def _():
            def send(h):
                top_copy(s, h, 0).start()
                top_copy(s, h, 1).start()

            halves(send)

    def pass_top(s):
        @pl.when(jnp.logical_not(head))
        def _():
            def onwards(h):
                top_copy(s, h, 0).wait_recv()

                @pl.when(onward)
                def _():
                    top_copy(s, h, 0).start()

                @pl.when(backward)
                def _():
                    top_copy(s, h, 1).start()

            halves(onwards)

        def to_others(h):
            for k in (1, 3, 2):
                top_other(s, h, k).start()

        halves(to_others)

    def pass_on(s):
        @pl.when(inner)
        def _():
            left_row_wait(s)

        for k in (1, 3, 2):
            left_other(s, k).start()

        @pl.when(col != 1)
        def _():
            left_core(s, 0).start()

        @pl.when(inner)
        def _():
            gather_copy(s, 0, 0).wait_recv()
            gather_pass(s, 0).start()

        gather_copy(s, 1, 1).wait_recv()
        gather_pass(s, 1).start()
        for k in (1, 3, 2):
            left_other(s, k).wait_recv()
            left_core(s, LAYERS - k).start()

    def lower_panel(s):
        n = THINS[s]

        @pl.when(inner)
        def _():
            left_core(s, 0).wait_recv()

        for k in range(1, LAYERS):
            left_core(s, k).wait_recv()
        rows = []
        for q in range(LAYERS):
            for i2 in range(2):
                rows.append(jnp.concatenate([b.left[s][q, 2 * j + i2] for j in range(4)], axis=1))
        hi, lo = split(jnp.concatenate(rows, axis=0))
        lower = dot(hi, b.inv_u[...]) + dot(lo, b.inv_u[...])
        b.low[s][...] = lower
        hi, lo = split(lower)
        b.low_hi[s][...] = hi
        b.low_lo[s][...] = lo

    def upper_panel(s):
        n = THINS[s]

        def arrived(h):
            for k in (1, 3, 2):
                top_other(s, h, k).wait_recv()

        halves(arrived)

        def add(c, carry):
            at = pl.ds(pl.multiple_of(c * 256, 256), 256)
            strips = [b.top[s][2 * c + h].reshape(4 * n, BLOCK) for h in range(2)]
            hi, lo = split(jnp.concatenate(strips, axis=1))
            inv = b.inv_lp[:, pl.ds(4 * STARTS[s], 4 * n)]
            term = dot(inv, hi) + dot(inv, lo)
            if s == 0:
                b.up[:, at] = term
            elif s < SLICES - 1:
                b.up[:, at] += term
            else:
                total = b.up[:, at] + term
                b.up[:, at] = total
                hi, lo = split(total)
                b.up_hi[:, at] = hi
                b.up_lo[:, at] = lo
            return carry

        lax.fori_loop(0, 4, add, 0)

    spread_extras(0)
    for s in range(SLICES):
        for k in range(LAYERS):
            core_copy(s, k).wait_recv()

        def slice_wait(k, carry):
            slice_copy(k, s).wait_recv()
            return carry

        lax.fori_loop(1, OWNERS, slice_wait, 0)
        add_up(s)
        for op in relay_out(s) + plain_out(s):
            op.start()
        if s == 0:

            @pl.when(inner)
            def _():
                sep_whole(0).wait()

            @pl.when(edge)
            def _():
                for j in range(4):
                    sep_edge(j).wait()

            sep_whole(1).wait()
        if s + AHEAD < SLICES:
            send_slice(s + AHEAD)
        if s + 1 < SLICES:
            spread_extras(s + 1)
        last = s == SLICES - 1
        if last:
            for t in range(s):
                top_out(t)
        if s >= 1:
            pass_on(s - 1)
        combine(s)
        if last:
            for t in range(s):
                pass_top(t)
        reduce(s)
        if last:
            top_out(s)
        if s >= 2:
            lower_panel(s - 2)
    pass_on(SLICES - 1)
    pass_top(SLICES - 1)
    lower_panel(SLICES - 2)
    for s in range(SLICES - 1):
        upper_panel(s)
    lower_panel(SLICES - 1)
    upper_panel(SLICES - 1)

    def out_copy(s):
        return [
            pltpu.make_async_copy(
                b.result[s].at[i], out_ref.at[pl.ds(i * BLOCK + STARTS[s], THINS[s])], b.out_sem.at[s, i]
            )
            for i in range(8)
        ]

    @pl.when(jnp.logical_and(edge, head))
    def _():
        rows = []
        for s in range(SLICES):
            for q in range(2):
                for i2 in range(2):
                    rows.append(jnp.concatenate([b.left[s][q, 2 * j + i2] for j in range(4)], axis=1))
        whole = jnp.concatenate(rows, axis=0)
        first, _ = split(whole)
        second, third = split(whole - first.astype(F32))
        order = b.perm[...].astype(F32).T.astype(BF16)
        b.up[:, 0:512] = dot(order, first) + dot(order, second) + dot(order, third)

    for s in range(SLICES):
        n = THINS[s]

        @pl.when(inner)
        def _():
            gather_copy(s, 0, 1).wait_recv()
            gather_pass(s, 0).wait_recv()

        gather_copy(s, 1, 0).wait_recv()
        gather_pass(s, 1).wait_recv()

        def trail(c, carry):
            at = pl.ds(pl.multiple_of(c * 256, 256), 256)
            hi, u_hi = b.low_hi[s][...], b.up_hi[:, at]
            change = dot(hi, u_hi) + (dot(b.low_lo[s][...], u_hi) + dot(hi, b.up_lo[:, at]))
            pieces = [b.piece[s][2 * c + h].reshape(8 * n, BLOCK) for h in range(2)]
            b.result[s][:, :, at] = (jnp.concatenate(pieces, axis=1) - change).reshape(8, n, 256)

            @pl.when(head)
            def _():
                for i in range(4):
                    b.result[s][i, :, at] = b.up[pl.ds(i * BLOCK + STARTS[s], n), at]

            return carry

        lax.fori_loop(0, 4, trail, 0)

        @pl.when(edge)
        def _():
            lower = b.low[s][...].reshape(8, n, 512)
            b.result[s][4:8, :, 0:512] = lower[4:8]

            @pl.when(jnp.logical_not(head))
            def _():
                b.result[s][0:4, :, 0:512] = lower[0:4]

        for op in out_copy(s):
            op.start()

    for s in range(SLICES):
        def sent(k, carry):
            slice_copy(k, s).wait_send()
            return carry

        lax.fori_loop(1, OWNERS, sent, 0)
        for op in relay_out(s) + plain_out(s) + comb_out(s):
            op.wait_send()
        for k in range(1, LAYERS):
            row_copy(s, k).wait_send()
            left_other(s, k).wait_send()
            left_core(s, k).wait_send()
        for k in range(LAYERS):
            core_copy(s, k).wait_send()

        @pl.when(col != 1)
        def _():
            left_core(s, 0).wait_send()

        @pl.when(edge)
        def _():
            for k in range(1, GRID):
                left_row(s, k).wait_send()

        def gone(h):
            @pl.when(jnp.logical_or(head, onward))
            def _():
                top_copy(s, h, 0).wait_send()

            @pl.when(jnp.logical_or(head, backward))
            def _():
                top_copy(s, h, 1).wait_send()

            for k in range(1, LAYERS):
                top_other(s, h, k).wait_send()
            for d in range(2):
                gather_copy(s, h, d).wait_send()
            gather_pass(s, h).wait_send()

        halves(gone)
    for h in range(1, 5):
        for op in ring_copies(h):
            op.wait_send()
    for k in range(1, LAYERS):
        peak_copy(k).wait()
        row_table(k).wait_send()
    for k in range(LAYERS):
        core_table(k).wait_send()
    peak_ref[...] = jnp.max(b.peak_buf[...], axis=0)
    for s in range(SLICES):
        for op in out_copy(s):
            op.wait()


def fused(owners, spots, left, right, separator, inverses, pivots):
    vmem = pl.BlockSpec(memory_space=pltpu.VMEM)
    hbm = pl.BlockSpec(memory_space=pl.ANY)
    return pl.pallas_call(
        fused_kernel,
        out_shape=(jax.ShapeDtypeStruct((8 * BLOCK, 1024), F32), jax.ShapeDtypeStruct((8, BLOCK), I32)),
        in_specs=[vmem, vmem, vmem, vmem, hbm, vmem, vmem],
        out_specs=(hbm, vmem),
        scratch_shapes=scratch_shapes(),
        compiler_params=pltpu.CompilerParams(
            collective_id=0, has_side_effects=True, vmem_limit_bytes=56 * 1024 * 1024
        ),
    )(owners, spots, left, right, separator, inverses, pivots)


def per_device(separator, left_factor, right_factor, owners, spots, pivot_order, panel_inverses):
    result, peak = fused(
        owners[:, 0][None, :], spots[None, :], left_factor, right_factor, separator, panel_inverses, pivot_order[None, :]
    )
    return lax.cond(
        peak[0, BLOCK - 1] > 1,
        lambda: general(separator, left_factor, right_factor, owners, spots, pivot_order, panel_inverses),
        lambda: result,
    )


def solution(mesh):
    in_specs = (
        P("prow", "pcol"),
        P(("layer", "prow", "pcol"), None, None),
        P(("layer", "prow", "pcol"), None, None),
        P(("layer", "prow", "pcol"), None),
        P(("layer", "prow", "pcol")),
        P(),
        P(),
    )
    return jax.shard_map(
        per_device, mesh=mesh, in_specs=in_specs, out_specs=P("prow", "pcol"), check_vma=False
    )
```

```python
import functools

import jax
import jax.numpy as jnp
from jax import lax
from jax.experimental import pallas as pl
from jax.experimental.pallas import tpu as pltpu
from jax.sharding import PartitionSpec as P

MESH = pl.DeviceIdType.MESH
GRID = 8
LAYERS = 4
OWNERS = GRID * GRID
BLOCK = 128
THINS = (32, 32, 32, 32)
STARTS = tuple(sum(THINS[:s]) for s in range(len(THINS)))
SLICES = len(THINS)
AHEAD = 2
EARLY = 16
F32 = jnp.float32
BF16 = jnp.bfloat16
I32 = jnp.int32


def split(x):
    high = x.astype(BF16)
    return high, (x - high.astype(F32)).astype(BF16)


def dot(a, b):
    return jnp.dot(a, b, preferred_element_type=F32)


def down(x):
    return jnp.sum(x, axis=0, keepdims=True)


def across(x):
    return jnp.sum(x, axis=1, keepdims=True)


def wide(x):
    return jnp.broadcast_to(x, (x.shape[0], BLOCK))


def exchange_kernel(
    index_ref, table_ref, left_ref, right_ref, recv_ref, tables_ref,
    out_buf, table_buf, send_sem, recv_sem, own_sem, table_send, table_recv,
):
    layer, row, col = lax.axis_index("layer"), lax.axis_index("prow"), lax.axis_index("pcol")
    me = row * GRID + col

    def place(k):
        return (row + k % GRID) % GRID, (col + k // GRID) % GRID

    barrier = pltpu.get_barrier_semaphore()

    def greet(k, carry):
        r, c = place(k)
        pl.semaphore_signal(barrier, inc=1, device_id=(layer, r, c), device_id_type=MESH)
        return carry

    lax.fori_loop(1, OWNERS, greet, 0)

    def product(k):
        r, c = place(k)
        for t in range(2):
            u = index_ref[t * OWNERS + r * GRID + c]
            out_buf[k, t] = jnp.dot(left_ref[u], right_ref[u], preferred_element_type=F32)

    def copy(k):
        r, c = place(k)
        return pltpu.make_async_remote_copy(
            src_ref=out_buf.at[k],
            dst_ref=recv_ref.at[me],
            send_sem=send_sem.at[k],
            recv_sem=recv_sem.at[k],
            device_id=(layer, r, c),
            device_id_type=MESH,
        )

    def table_copy(k):
        r, c = place(k)
        return pltpu.make_async_remote_copy(
            src_ref=table_ref,
            dst_ref=table_buf.at[me],
            send_sem=table_send.at[k],
            recv_sem=table_recv.at[k],
            device_id=(layer, r, c),
            device_id_type=MESH,
        )

    pl.semaphore_wait(barrier, OWNERS - 1)

    def send(k, carry):
        product(k)
        copy(k).start()
        table_copy(k).start()
        return carry

    lax.fori_loop(1, OWNERS, send, 0)
    product(0)
    own = pltpu.make_async_copy(out_buf.at[0], recv_ref.at[me], own_sem)
    own.start()
    table_buf[me] = table_ref[...]

    def finish(k, carry):
        table_copy(k).wait()
        copy(k).wait()
        return carry

    lax.fori_loop(1, OWNERS, finish, 0)
    own.wait()
    tables_ref[...] = table_buf[...]


def exchange(index, table, left, right):
    vmem = pl.BlockSpec(memory_space=pltpu.VMEM)
    dma = pltpu.SemaphoreType.DMA
    return pl.pallas_call(
        exchange_kernel,
        out_shape=(
            jax.ShapeDtypeStruct((OWNERS, 2, BLOCK, BLOCK), F32),
            jax.ShapeDtypeStruct((OWNERS, 8, BLOCK), I32),
        ),
        in_specs=[pl.BlockSpec(memory_space=pltpu.SMEM), vmem, vmem, vmem],
        out_specs=(pl.BlockSpec(memory_space=pl.ANY), vmem),
        scratch_shapes=[
            pltpu.VMEM((OWNERS, 2, BLOCK, BLOCK), F32),
            pltpu.VMEM((OWNERS, 8, BLOCK), I32),
            dma((OWNERS,)),
            dma((OWNERS,)),
            dma,
            dma((OWNERS,)),
            dma((OWNERS,)),
        ],
        compiler_params=pltpu.CompilerParams(
            collective_id=1, has_side_effects=True, vmem_limit_bytes=32 * 1024 * 1024
        ),
    )(index, table, left, right)


def scatter_kernel(slot_ref, recv_ref, out_ref):
    step = pl.program_id(0)

    @pl.when(step == 0)
    def _():
        out_ref[...] = jnp.zeros_like(out_ref)

    def add(k, carry):
        slot = slot_ref[step * 8 + k]

        @pl.when(slot < 64)
        def _():
            out_ref[slot] += recv_ref[k]

        return carry

    lax.fori_loop(0, 8, add, 0)


def scatter(slots, recv):
    return pl.pallas_call(
        scatter_kernel,
        out_shape=jax.ShapeDtypeStruct((64, BLOCK, BLOCK), F32),
        grid=(2 * OWNERS // 8,),
        in_specs=[
            pl.BlockSpec(memory_space=pltpu.SMEM),
            pl.BlockSpec((8, BLOCK, BLOCK), lambda i: (i, 0, 0)),
        ],
        out_specs=pl.BlockSpec((64, BLOCK, BLOCK), lambda i: (0, 0, 0)),
        compiler_params=pltpu.CompilerParams(vmem_limit_bytes=24 * 1024 * 1024),
    )(slots, recv)


def panel_kernel(
    dense_ref, sep_ref, inv_ref, pivot_ref, out_ref,
    sep_buf, relay, comb, plain, red, top, left, low, up_hi, up_lo, up, perm, inv_lp, inv_u,
    sep_sem, rs_send, rs_recv, top_send, top_recv, ly_send, ly_recv, lx_send, lx_recv, lc_send, lc_recv,
    ag_send, ag_recv, fw_send, fw_recv, out_sem,
):
    layer, row, col = lax.axis_index("layer"), lax.axis_index("prow"), lax.axis_index("pcol")
    core = col % 2
    nxt, prv, opp = (layer + 1) % LAYERS, (layer + 3) % LAYERS, (layer + 2) % LAYERS
    edge = col == 0
    head = row == 0
    half = 4 * BLOCK

    def remote(src, dst, send, recv, device):
        return pltpu.make_async_remote_copy(
            src_ref=src, dst_ref=dst, send_sem=send, recv_sem=recv, device_id=device, device_id_type=MESH
        )

    to_nxt, to_prv, to_opp = (nxt, row, col), (prv, row, col), (opp, row, col)
    up_row, down_row = (row + 1) % GRID, (row + GRID - 1) % GRID

    barrier = pltpu.get_barrier_semaphore()
    for device in (to_nxt, to_prv, to_opp, (layer, up_row, col), (layer, down_row, col)):
        pl.semaphore_signal(barrier, inc=1, device_id=device, device_id_type=MESH)
    for k in range(1, GRID):
        pl.semaphore_signal(barrier, inc=1, device_id=(layer, row, (col + k) % GRID), device_id_type=MESH)

    def sep_first():
        return pltpu.make_async_copy(
            sep_ref.at[:, pl.ds(pl.multiple_of(layer * 2 * BLOCK, BLOCK), BLOCK)], sep_buf.at[0], sep_sem.at[0]
        )

    def sep_edge(j):
        return pltpu.make_async_copy(
            sep_ref.at[pl.ds(pl.multiple_of(layer * 256, 256), 256), pl.ds(j * BLOCK, BLOCK)],
            sep_buf.at[0, pl.ds(j * 256, 256)],
            sep_sem.at[2 + j],
        )

    def column(q, h):
        normal = 2 * q + h
        return pl.multiple_of(jnp.where(edge, 4 + q, normal) * BLOCK, BLOCK)

    sep_second = pltpu.make_async_copy(
        sep_ref.at[:, pl.ds(column(layer, 1), BLOCK)], sep_buf.at[1], sep_sem.at[1]
    )
    sep_second.start()

    @pl.when(jnp.logical_not(edge))
    def _():
        sep_first().start()

    @pl.when(edge)
    def _():
        for j in range(4):
            sep_edge(j).start()

    pl.semaphore_wait(barrier, 5 + GRID - 1)

    relay_out = [
        remote(dense_ref.at[2 * opp], relay.at[0], rs_send.at[0], rs_recv.at[0], to_nxt),
        remote(dense_ref.at[2 * opp + 1], relay.at[1], rs_send.at[1], rs_recv.at[1], to_prv),
    ]
    plain_out = [
        remote(dense_ref.at[2 * prv], plain.at[0], rs_send.at[2], rs_recv.at[2], to_prv),
        remote(dense_ref.at[2 * nxt + 1], plain.at[1], rs_send.at[3], rs_recv.at[3], to_nxt),
    ]
    comb_out = [
        remote(relay.at[0], comb.at[0], rs_send.at[4], rs_recv.at[4], to_nxt),
        remote(relay.at[1], comb.at[1], rs_send.at[5], rs_recv.at[5], to_prv),
    ]
    relay_out[0].start()
    relay_out[1].start()
    plain_out[1].start()
    plain_out[0].start()

    inv = inv_ref[...]
    rows_at = lax.broadcasted_iota(jnp.int32, (half, half), 0)
    cols_at = lax.broadcasted_iota(jnp.int32, (half, half), 1)
    inv_f = inv.astype(F32)
    lower_inverse = jnp.where(rows_at > cols_at, inv_f, jnp.where(rows_at == cols_at, 1.0, 0.0))
    inv_u[...] = jnp.where(rows_at <= cols_at, inv_f, 0.0).astype(jnp.bfloat16)
    perm[...] = jnp.where(pivot_ref[...] == cols_at, 1.0, 0.0).astype(jnp.bfloat16)
    inv_lp[...] = dot(lower_inverse.astype(jnp.bfloat16), perm[...]).astype(jnp.bfloat16)

    relay_out[0].wait_recv()
    relay[0] += dense_ref[2 * nxt]
    comb_out[0].start()
    relay_out[1].wait_recv()
    relay[1] += dense_ref[2 * prv + 1]
    comb_out[1].start()

    @pl.when(jnp.logical_not(edge))
    def _():
        sep_first().wait()

    @pl.when(edge)
    def _():
        for j in range(4):
            sep_edge(j).wait()

    sep_second.wait()
    for h in range(2):
        plain_out[h].wait_recv()
        red[h] = sep_buf[h] - (dense_ref[2 * layer + h] + plain[h])
    for h in range(2):
        comb_out[h].wait_recv()
        red[h] -= comb[h]

    def top_copy(h, s, d):
        part = top.at[h, pl.ds(s * 256, 256)]
        return remote(
            part, part, top_send.at[d, h, s], top_recv.at[h, s],
            (layer, (up_row if d == 0 else down_row), col),
        )

    def top_wait(h, s):
        top_copy(h, s, 0).wait_recv()

    onward = jnp.logical_and(row >= 1, row <= 3)
    backward = row >= 6

    def for_top(action):
        for h in (1, 0):
            for s in range(2):
                if h == 1:
                    action(h, s)
                else:
                    pl.when(jnp.logical_not(edge))(functools.partial(action, h, s))

    @pl.when(head)
    def _():
        top[0] = red[0, :half]
        top[1] = red[1, :half]

        def action(h, s):
            top_copy(h, s, 0).start()
            top_copy(h, s, 1).start()

        for_top(action)

    @pl.when(jnp.logical_and(edge, jnp.logical_not(head)))
    def _():
        top[0] = jnp.zeros((half, BLOCK), F32)

    def left_y(k):
        c = (col + k) % GRID
        part = left.at[layer, pl.ds((c % 2) * half, half)]
        return remote(part, part, ly_send.at[k], ly_recv, (layer, row, c))

    @pl.when(edge)
    def _():
        left[layer] = red[0]
        for k in (2, 3, 6, 7, 4, 5, 1):
            left_y(k).start()

    @pl.when(jnp.logical_not(edge))
    def _():
        mine = left.at[layer, pl.ds(core * half, half)]
        remote(mine, mine, ly_send.at[0], ly_recv, (layer, row, (col + 1) % GRID)).wait_recv()

    def left_x(k):
        part = left.at[layer, pl.ds(core * half, half)]
        return remote(part, part, lx_send.at[k], lx_recv.at[k], ((layer + k) % LAYERS, row, col))

    def left_x_wait(k):
        part = left.at[(layer + LAYERS - k) % LAYERS, pl.ds(core * half, half)]
        remote(part, part, lx_send.at[k], lx_recv.at[k], ((layer + k) % LAYERS, row, col)).wait_recv()

    sibling = (layer, row, col + 1 - 2 * core)

    def left_c(k):
        part = left.at[(layer + k) % LAYERS, pl.ds(core * half, half)]
        return remote(part, part, lc_send.at[k], lc_recv.at[k], sibling)

    def left_c_wait(k):
        part = left.at[(layer + k) % LAYERS, pl.ds((1 - core) * half, half)]
        remote(part, part, lc_send.at[k], lc_recv.at[k], sibling).wait_recv()

    for k in (1, 3, 2):
        left_x(k).start()

    @pl.when(col != 1)
    def _():
        left_c(0).start()

    @pl.when(jnp.logical_not(head))
    def _():
        def action(h, s):
            top_wait(h, s)

            @pl.when(onward)
            def _():
                top_copy(h, s, 0).start()

            @pl.when(backward)
            def _():
                top_copy(h, s, 1).start()

        for_top(action)

    for k in (1, 3, 2):
        left_x_wait(k)
        left_c(LAYERS - k).start()

    top_both = jnp.concatenate([top[0], top[1]], axis=1)
    top_hi, top_lo = split(top_both)
    up[...] = dot(inv_lp[...], top_hi) + dot(inv_lp[...], top_lo)
    hi, lo = split(up[...])
    up_hi[...] = hi
    up_lo[...] = lo

    @pl.when(jnp.logical_not(edge))
    def _():
        left_c_wait(0)

    for k in range(1, LAYERS):
        left_c_wait(k)

    def send_part(r, h, d):
        return remote(
            red.at[h, pl.ds(pl.multiple_of(r * 256, 256), 256)],
            out_ref.at[pl.ds(pl.multiple_of(r * 256, 256), 256), pl.ds(column(layer, h), BLOCK)],
            ag_send.at[d, h, r], ag_recv.at[d, h, r], (to_nxt if d == 0 else to_prv),
        )

    def wait_part(r, h, d):
        send_part(r, h, d).wait_recv()

    def forward_part(r, d):
        q = prv if d == 0 else nxt
        part = out_ref.at[pl.ds(pl.multiple_of(r * 256, 256), 256), pl.ds(column(q, d), BLOCK)]
        return remote(part, part, fw_send.at[d, r], fw_recv.at[d, r], (to_nxt if d == 0 else to_prv))

    def compute(r, carry):
        at = pl.ds(pl.multiple_of(r * 256, 256), 256)
        quarter = left[r]
        rows = jnp.concatenate([quarter[256 * j : 256 * (j + 1)] for j in range(4)], axis=1)
        rows_hi, rows_lo = split(rows)
        lower = dot(rows_hi, inv_u[...]) + dot(rows_lo, inv_u[...])
        low[at] = lower
        l_hi, l_lo = split(lower)
        u_hi, u_lo = up_hi[...], up_lo[...]
        change = dot(l_hi, u_hi) + (dot(l_lo, u_hi) + dot(l_hi, u_lo))
        in_head = jnp.logical_and(head, r < 2)
        upper = up[pl.ds(pl.multiple_of((r % 2) * 256, 256), 256)]
        for h in range(2):
            cut = slice(h * BLOCK, (h + 1) * BLOCK)
            red[h, at] = jnp.where(in_head, upper[:, cut], red[h, at] - change[:, cut])

        @pl.when(jnp.logical_not(edge))
        def _():
            send_part(r, 0, 0).start()
            send_part(r, 0, 1).start()

        send_part(r, 1, 1).start()
        send_part(r, 1, 0).start()
        return carry

    lax.fori_loop(0, LAYERS, compute, 0)

    def own_part(h):
        return pltpu.make_async_copy(red.at[h], out_ref.at[:, pl.ds(column(layer, h), BLOCK)], out_sem.at[h])

    own_part(1).start()

    @pl.when(jnp.logical_not(edge))
    def _():
        own_part(0).start()

    lower_copy = pltpu.make_async_copy(low, out_ref.at[:, pl.ds(0, half)], out_sem.at[2])

    @pl.when(edge)
    def _():
        @pl.when(head)
        def _():
            quarters = []
            for q in range(2):
                quarters.append(jnp.concatenate([left[q, 256 * j : 256 * (j + 1)] for j in range(4)], axis=1))
            rows = jnp.concatenate(quarters, axis=0)
            first, rest = split(rows)
            second, third = split(rows - first.astype(F32))
            low[:half] = dot(perm[...], first) + dot(perm[...], second) + dot(perm[...], third)

        lower_copy.start()

    def pass_on(r, carry):
        @pl.when(jnp.logical_not(edge))
        def _():
            wait_part(r, 0, 0)
            forward_part(r, 0).start()

        wait_part(r, 1, 1)
        forward_part(r, 1).start()
        return carry

    lax.fori_loop(0, LAYERS, pass_on, 0)

    def finish(r, carry):
        @pl.when(jnp.logical_not(edge))
        def _():
            wait_part(r, 0, 1)
            forward_wait(r, 0)
            send_part(r, 0, 0).wait_send()
            send_part(r, 0, 1).wait_send()
            forward_part(r, 0).wait_send()

        wait_part(r, 1, 0)
        forward_wait(r, 1)
        send_part(r, 1, 0).wait_send()
        send_part(r, 1, 1).wait_send()
        forward_part(r, 1).wait_send()
        return carry

    def forward_wait(r, d):
        forward_part(r, d).wait_recv()

    lax.fori_loop(0, LAYERS, finish, 0)

    for op in relay_out + plain_out + comb_out:
        op.wait_send()

    def sent(h, s):
        @pl.when(jnp.logical_or(head, onward))
        def _():
            top_copy(h, s, 0).wait_send()

        @pl.when(jnp.logical_or(head, backward))
        def _():
            top_copy(h, s, 1).wait_send()

    for_top(sent)

    @pl.when(edge)
    def _():
        for k in range(1, GRID):
            left_y(k).wait_send()

    for k in range(1, LAYERS):
        left_x(k).wait_send()
        left_c(k).wait_send()

    @pl.when(col != 1)
    def _():
        left_c(0).wait_send()

    own_part(1).wait()

    @pl.when(jnp.logical_not(edge))
    def _():
        own_part(0).wait()

    @pl.when(edge)
    def _():
        lower_copy.wait()


def panel(dense, separator, inverses, pivots):
    rows, cols = separator.shape
    half = 4 * BLOCK
    vmem = pl.BlockSpec(memory_space=pltpu.VMEM)
    hbm = pl.BlockSpec(memory_space=pl.ANY)
    dma = pltpu.SemaphoreType.DMA
    strip = (2, rows, BLOCK)
    bf16 = jnp.bfloat16
    return pl.pallas_call(
        panel_kernel,
        out_shape=jax.ShapeDtypeStruct((rows, cols), F32),
        in_specs=[vmem, hbm, vmem, vmem],
        out_specs=hbm,
        scratch_shapes=[
            pltpu.VMEM(strip, F32),
            pltpu.VMEM(strip, F32),
            pltpu.VMEM(strip, F32),
            pltpu.VMEM(strip, F32),
            pltpu.VMEM(strip, F32),
            pltpu.VMEM((2, half, BLOCK), F32),
            pltpu.VMEM((LAYERS, rows, BLOCK), F32),
            pltpu.VMEM((rows, half), F32),
            pltpu.VMEM((half, 256), bf16),
            pltpu.VMEM((half, 256), bf16),
            pltpu.VMEM((half, 256), F32),
            pltpu.VMEM((half, half), bf16),
            pltpu.VMEM((half, half), bf16),
            pltpu.VMEM((half, half), bf16),
            dma((6,)),
            dma((6,)),
            dma((6,)),
            dma((2, 2, 2)),
            dma((2, 2)),
            dma((GRID,)),
            dma,
            dma((LAYERS,)),
            dma((LAYERS,)),
            dma((LAYERS,)),
            dma((LAYERS,)),
            dma((2, 2, LAYERS)),
            dma((2, 2, LAYERS)),
            dma((2, LAYERS)),
            dma((2, LAYERS)),
            dma((3,)),
        ],
        compiler_params=pltpu.CompilerParams(
            collective_id=2, has_side_effects=True, vmem_limit_bytes=40 * 1024 * 1024
        ),
    )(dense, separator, inverses, pivots)


def general(separator, left_factor, right_factor, owners, spots, pivot_order, panel_inverses):
    destination = owners[:, 0]
    counter = jnp.arange(OWNERS)
    same = destination[:, None] == destination[None, :]
    rank = jnp.sum(same & (counter[None, :] < counter[:, None]), axis=1)
    named = (destination[None, :] == jnp.arange(2 * OWNERS)[:, None] % OWNERS) & (
        rank[None, :] == jnp.arange(2 * OWNERS)[:, None] // OWNERS
    )
    index = jnp.sum(jnp.where(named, counter[None, :], 0), axis=1).astype(I32)
    placed = jnp.where(jnp.any(named, axis=1), jnp.sum(jnp.where(named, spots[None, :], 0), axis=1), 64)
    table = jnp.broadcast_to(placed.astype(I32)[None, :], (8, 2 * OWNERS))
    recv, tables = exchange(index, table, left_factor, right_factor)
    col = lax.axis_index("pcol")
    me = lax.axis_index("prow") * GRID + col
    arrived = lax.dynamic_index_in_dim(tables[:, 0, :].reshape(OWNERS, 2, OWNERS), me, 2, keepdims=False)
    spot = arrived.reshape(2 * OWNERS)
    i, j = spot // 8, spot % 8
    inside = jnp.where(j < 4, (i // 2) * 16 + j * 2 + i % 2, (2 * (j - 4) + 1) * 8 + i)
    slots = jnp.where(spot < 64, jnp.where(col == 0, inside, j * 8 + i), 64)
    dense = scatter(slots, recv.reshape(2 * OWNERS, BLOCK, BLOCK))
    return panel(dense.reshape(8, 1024, BLOCK), separator, panel_inverses, pivot_order[:, None])


SCRATCH = (
    ("mains", "each", lambda n: ((2 * GRID, GRID, n, BLOCK), F32)),
    ("dense", "each", lambda n: ((OWNERS, n, BLOCK), F32)),
    ("relay", "each", lambda n: ((2, 8, n, BLOCK), F32)),
    ("comb", "each", lambda n: ((2, 8, n, BLOCK), F32)),
    ("plain", "each", lambda n: ((2, 8, n, BLOCK), F32)),
    ("piece", "each", lambda n: ((8, 8, n, BLOCK), F32)),
    ("top", "each", lambda n: ((8, 4, n, BLOCK), F32)),
    ("left", "each", lambda n: ((LAYERS, 8, n, BLOCK), F32)),
    ("low", "each", lambda n: ((8 * n, 512), F32)),
    ("low_hi", "each", lambda n: ((8 * n, 512), BF16)),
    ("low_lo", "each", lambda n: ((8 * n, 512), BF16)),
    ("result", "each", lambda n: ((8, n, 1024), F32)),
    ("ring", "one", ((GRID, BLOCK, BLOCK), F32)),
    ("out_buf", "one", ((OWNERS, BLOCK, BLOCK), F32)),
    ("table_buf", "one", ((GRID, GRID, 8, BLOCK), I32)),
    ("peak_buf", "one", ((LAYERS, 8, BLOCK), I32)),
    ("index_buf", "one", ((8, BLOCK), I32)),
    ("sorted_buf", "one", ((8, BLOCK), I32)),
    ("running", "one", ((2 * OWNERS, max(THINS), BLOCK), F32)),
    ("sep_buf", "one", ((2, 1024, BLOCK), F32)),
    ("up", "one", ((512, 1024), F32)),
    ("up_hi", "one", ((512, 1024), BF16)),
    ("up_lo", "one", ((512, 1024), BF16)),
    ("inv_lp", "one", ((512, 512), BF16)),
    ("inv_u", "one", ((512, 512), BF16)),
    ("perm", "one", ((512, 512), BF16)),
    ("index_mem", "smem", ((8, BLOCK), I32)),
    ("sorted_mem", "smem", ((8, BLOCK), I32)),
    ("a_sem", "sem", (2, SLICES, OWNERS)),
    ("p_sem", "sem", (2, LAYERS)),
    ("z_sem", "sem", (2, 2, 2, 5)),
    ("y_sem", "sem", (2, SLICES, LAYERS)),
    ("c_sem", "sem", (2, SLICES, LAYERS)),
    ("ty_sem", "sem", (2, LAYERS)),
    ("tc_sem", "sem", (2, LAYERS)),
    ("mem_sem", "sem", (2,)),
    ("sep_sem", "sem", (6,)),
    ("rs_sem", "sem", (2, SLICES, 6)),
    ("ag_sem", "sem", (2, SLICES, 2, 2)),
    ("fw_sem", "sem", (2, SLICES, 2)),
    ("top_sem", "sem", (3, SLICES, 2)),
    ("tx_sem", "sem", (2, SLICES, 2, LAYERS)),
    ("ly_sem", "sem", (SLICES, 1 + GRID)),
    ("lx_sem", "sem", (2, SLICES, LAYERS)),
    ("lc_sem", "sem", (2, SLICES, LAYERS)),
    ("out_sem", "sem", (SLICES, 8)),
)


def scratch_shapes():
    shapes = []
    for _, kind, what in SCRATCH:
        if kind == "each":
            shapes += [pltpu.VMEM(*what(n)) for n in THINS]
        elif kind == "one":
            shapes.append(pltpu.VMEM(*what))
        elif kind == "smem":
            shapes.append(pltpu.SMEM(*what))
        else:
            shapes.append(pltpu.SemaphoreType.DMA(what))
    return shapes


class Scratch:
    def __init__(self, refs):
        at = 0
        for name, kind, _ in SCRATCH:
            if kind == "each":
                setattr(self, name, refs[at : at + SLICES])
                at += SLICES
            else:
                setattr(self, name, refs[at])
                at += 1


def fused_kernel(
    owners_ref, spots_ref, left_ref, right_ref, sep_ref, inv_ref, pivot_ref, out_ref, peak_ref, *refs
):
    b = Scratch(refs)
    layer, row, col = lax.axis_index("layer"), lax.axis_index("prow"), lax.axis_index("pcol")
    me = row * GRID + col
    core = col % 2
    nxt, prv, opp = (layer + 1) % LAYERS, (layer + 3) % LAYERS, (layer + 2) % LAYERS
    edge = col == 0
    inner = jnp.logical_not(edge)
    head = row == 0
    up_row, down_row = (row + 1) % GRID, (row + GRID - 1) % GRID
    to_nxt, to_prv = (nxt, row, col), (prv, row, col)
    sibling = (layer, row, col + 1 - 2 * core)

    def remote(src, dst, sems, device):
        return pltpu.make_async_remote_copy(
            src_ref=src, dst_ref=dst, send_sem=sems[0], recv_sem=sems[1], device_id=device, device_id_type=MESH
        )

    def pair(sem, *at):
        return sem.at[(0, *at)], sem.at[(1, *at)]

    def place(k):
        return (row + k % GRID) % GRID, (col + k // GRID) % GRID

    def other(k):
        return ((layer + k) % LAYERS, row, col)

    def column(q, h):
        return jnp.where(edge, 4 + q, 2 * q + h)

    barrier = pltpu.get_barrier_semaphore()

    def greet(k, carry):
        r, c = place(k)
        pl.semaphore_signal(barrier, inc=1, device_id=(layer, r, c), device_id_type=MESH)
        return carry

    lax.fori_loop(1, OWNERS, greet, 0)
    for k in range(1, LAYERS):
        pl.semaphore_signal(barrier, inc=1, device_id=other(k), device_id_type=MESH)

    def sep_whole(h):
        return pltpu.make_async_copy(
            sep_ref.at[:, pl.ds(pl.multiple_of(column(layer, h) * BLOCK, BLOCK), BLOCK)],
            b.sep_buf.at[h],
            b.sep_sem.at[h],
        )

    def sep_edge(j):
        return pltpu.make_async_copy(
            sep_ref.at[pl.ds(pl.multiple_of(layer * 256, 256), 256), pl.ds(j * BLOCK, BLOCK)],
            b.sep_buf.at[0, pl.ds(j * 256, 256)],
            b.sep_sem.at[2 + j],
        )

    sep_whole(1).start()

    @pl.when(inner)
    def _():
        sep_whole(0).start()

    @pl.when(edge)
    def _():
        for j in range(4):
            sep_edge(j).start()

    lane = lax.broadcasted_iota(I32, (OWNERS, BLOCK), 1)
    line = lax.broadcasted_iota(I32, (OWNERS, BLOCK), 0)
    lane_row = lax.broadcasted_iota(I32, (1, BLOCK), 1)
    owner_all = jnp.broadcast_to(jnp.concatenate([owners_ref[...], spots_ref[...]], axis=1), (BLOCK, BLOCK))
    owner_row, both = owner_all[:OWNERS], owner_all.T
    owner_col, spot_col = both[:OWNERS], both[OWNERS:]
    rank = wide(across(jnp.where((owner_row == owner_col) & (lane < line), 1, 0)))
    hit = (owner_col == lane) & (rank == 0)
    index_row = down(jnp.where(hit, line, 0))
    spot_row = down(jnp.where(hit, spot_col, 0))
    hits = down(jnp.where(hit, 1, 0))
    second = rank == 1
    count_row = down(jnp.where(second, 1, 0))
    chosen = jnp.min(jnp.where(second, line, OWNERS), axis=0, keepdims=True)
    pick = line == chosen
    code_row = down(jnp.where(pick, owner_col * 64 + spot_col, 0))
    chosen_row = down(jnp.where(pick, line, 0))
    index_row = jnp.where(lane_row < OWNERS, index_row, chosen_row)
    spot_row = jnp.where(hits > 0, spot_row, 64)
    code_row = jnp.where(count_row > 0, code_row, -1)
    table_row = jnp.where(lane_row < OWNERS, spot_row, jnp.where(lane_row == OWNERS, code_row, count_row))
    b.table_buf[row, col] = jnp.broadcast_to(table_row, (8, BLOCK))
    b.index_buf[...] = jnp.broadcast_to(index_row, (8, BLOCK))
    to_mem = pltpu.make_async_copy(b.index_buf, b.index_mem, b.mem_sem.at[0])
    to_mem.start()
    to_mem.wait()

    def multiply(u):
        return dot(left_ref[u], right_ref[u])

    def product(k):
        r, c = place(k)
        b.out_buf[k] = multiply(b.index_mem[0, r * GRID + c])

    def slice_copy(k, s):
        r, c = place(k)
        return remote(
            b.out_buf.at[k, pl.ds(STARTS[s], THINS[s])], b.mains[s].at[row, col], pair(b.a_sem, s, k), (layer, r, c)
        )

    def peak_copy(k):
        return remote(b.peak_buf.at[0], b.peak_buf.at[k], pair(b.p_sem, k), other(k))

    def ring_copies(h):
        copies = []
        for d in range(2 if h <= 3 else 1):
            source = (row + GRID - h + 1) % GRID if d == 0 else (row + h - 1) % GRID
            device = (layer, (up_row if d == 0 else down_row), col)
            block, table = b.ring.at[source], b.table_buf.at[source, col]
            copies.append(remote(block, block, pair(b.z_sem, 0, d, h), device))
            copies.append(remote(table, table, pair(b.z_sem, 1, d, h), device))
        return copies

    def row_copy(s, k):
        return remote(
            b.ring.at[:, pl.ds(STARTS[s], THINS[s])],
            b.mains[s].at[pl.ds(GRID, GRID), col],
            pair(b.y_sem, s, k),
            (layer, row, (col + 2 * k) % GRID),
        )

    def core_copy(s, k):
        part = b.mains[s].at[pl.ds(GRID, GRID), (col + GRID - 2 * k) % GRID]
        return remote(part, part, pair(b.c_sem, s, k), sibling)

    def row_table(k):
        part = b.table_buf.at[:, col]
        return remote(part, part, pair(b.ty_sem, k), (layer, row, (col + 2 * k) % GRID))

    def core_table(k):
        part = b.table_buf.at[:, (col + GRID - 2 * k) % GRID]
        return remote(part, part, pair(b.tc_sem, k), sibling)

    def early(k, carry):
        product(k)
        return carry

    b.ring[row] = multiply(b.index_mem[0, OWNERS])
    lax.fori_loop(1, 1 + EARLY, early, 0, unroll=4)
    pl.semaphore_wait(barrier, OWNERS - 1 + LAYERS - 1)

    def first_slice(k, carry):
        slice_copy(k, 0).start()
        product(k + EARLY)
        return carry

    def send_slice(s, first=1):
        def send(k, carry):
            slice_copy(k, s).start()
            return carry

        lax.fori_loop(first, OWNERS, send, 0)

    for op in ring_copies(1):
        op.start()
    lax.fori_loop(1, 9, first_slice, 0)
    for h in range(1, 4):
        for op in ring_copies(h):
            op.wait_recv()
        for op in ring_copies(h + 1):
            op.start()
        lax.fori_loop(1 + 8 * h, 9 + 8 * h, first_slice, 0)
    for op in ring_copies(4):
        op.wait_recv()
    for k in (1, 3, 2):
        row_table(k).start()
    core_table(0).start()
    for s in range(SLICES):
        for k in (1, 3, 2):
            row_copy(s, k).start()
        for r in range(GRID):
            b.mains[s][GRID + r, col] = b.ring[r, pl.ds(STARTS[s], THINS[s])]
        core_copy(s, 0).start()
    lax.fori_loop(33, OWNERS - EARLY, first_slice, 0)
    send_slice(0, OWNERS - EARLY)
    own = multiply(b.index_mem[0, me])
    for s in range(SLICES):
        b.mains[s][row, col] = own[STARTS[s] : STARTS[s] + THINS[s]]
    for s in range(1, AHEAD):
        send_slice(s)

    inv = inv_ref[...].astype(F32)
    rows_at = lax.broadcasted_iota(I32, (512, 512), 0)
    cols_at = lax.broadcasted_iota(I32, (512, 512), 1)
    lower_inverse = jnp.where(rows_at > cols_at, inv, jnp.where(rows_at == cols_at, 1.0, 0.0)).astype(BF16)
    b.inv_u[...] = jnp.where(rows_at <= cols_at, inv, 0.0).astype(BF16)
    for s in range(SLICES):
        n = 4 * THINS[s]
        at = lax.broadcasted_iota(I32, (n, 512), 0)
        source = (at // THINS[s]) * BLOCK + STARTS[s] + at % THINS[s]
        b.perm[pl.ds(4 * STARTS[s], n)] = jnp.where(pivot_ref[...] == source, 1.0, 0.0).astype(BF16)
    b.inv_lp[...] = lax.dot_general(
        lower_inverse, b.perm[...], (((1,), (1,)), ((), ())), preferred_element_type=F32
    ).astype(BF16)

    for k in (1, 3, 2):
        row_table(k).wait_recv()
        core_table(k).start()
    for k in range(LAYERS):
        core_table(k).wait_recv()
    tables = b.table_buf[...].reshape(OWNERS, 8, BLOCK)
    b.peak_buf[0] = jnp.max(tables, axis=0)
    for k in range(1, LAYERS):
        peak_copy(k).start()
    tables = tables[:, 0, :]
    mine = across(jnp.where(lane == me, tables, 0))
    code = across(jnp.where(lane == OWNERS, tables, 0))
    extra = jnp.where((code >= 0) & ((code >> 6) == me), code & 63, 64)
    spot = jnp.concatenate([mine, extra], axis=0)
    i, j = spot >> 3, spot & 7
    inside = jnp.where(j < 4, (i >> 1) * 16 + j * 2 + (i & 1), (2 * (j - 4) + 1) * 8 + i)
    slot_col = wide(jnp.where(spot < 64, jnp.where(edge, inside, j * 8 + i), 64))
    slot_row = slot_col.T
    line2 = lax.broadcasted_iota(I32, (BLOCK, BLOCK), 0)
    lane2 = lax.broadcasted_iota(I32, (BLOCK, BLOCK), 1)
    ahead = (slot_row < slot_col) | ((slot_row == slot_col) & (lane2 < line2))
    rank2 = wide(across(jnp.where(ahead, 1, 0)))
    order_row = down(jnp.where(rank2 == lane2, line2, 0))
    slots_row = down(jnp.where(rank2 == lane2, slot_col, 0))
    before_row = down(jnp.where(rank2 == lane2 - 1, slot_col, 0))
    same_row = jnp.where((slots_row == before_row) & (lane_row > 0), 1, 0)
    last_row = jnp.maximum(down(jnp.where(slot_col <= lane2, 1, 0)) - 1, 0)
    filled_row = jnp.where(down(jnp.where(slot_col == lane2, 1, 0)) > 0, 1, 0)
    b.sorted_buf[0:1] = order_row
    b.sorted_buf[1:2] = same_row
    b.sorted_buf[2:3] = last_row
    b.sorted_buf[3:4] = filled_row
    b.sorted_buf[4:8] = jnp.zeros((4, BLOCK), I32)
    to_sorted = pltpu.make_async_copy(b.sorted_buf, b.sorted_mem, b.mem_sem.at[1])
    to_sorted.start()
    to_sorted.wait()

    def spread_extras(s):
        for k in (1, 3, 2):
            row_copy(s, k).wait_recv()
            core_copy(s, k).start()

    def add_up(s):
        thin = pl.ds(0, THINS[s])

        def run(k, total):
            e = b.sorted_mem[0, k]
            total = b.mains[s][e >> 3, e & 7] + jnp.where(b.sorted_mem[1, k] == 1, total, 0.0)
            b.running[k, thin] = total
            return total

        lax.fori_loop(0, 2 * OWNERS, run, jnp.zeros((THINS[s], BLOCK), F32), unroll=8)

        def settle(k, carry):
            value = b.running[b.sorted_mem[2, k], thin]
            b.dense[s][k] = jnp.where(b.sorted_mem[3, k] == 1, value, 0.0)
            return carry

        lax.fori_loop(0, OWNERS, settle, 0, unroll=8)

    def strip(s, q):
        return b.dense[s].at[pl.ds(pl.multiple_of(8 * q, 8), 8)]

    def relay_out(s):
        return [
            remote(strip(s, 2 * opp), b.relay[s].at[0], pair(b.rs_sem, s, 0), to_nxt),
            remote(strip(s, 2 * opp + 1), b.relay[s].at[1], pair(b.rs_sem, s, 1), to_prv),
        ]

    def plain_out(s):
        return [
            remote(strip(s, 2 * prv), b.plain[s].at[0], pair(b.rs_sem, s, 2), to_prv),
            remote(strip(s, 2 * nxt + 1), b.plain[s].at[1], pair(b.rs_sem, s, 3), to_nxt),
        ]

    def comb_out(s):
        return [
            remote(b.relay[s].at[0], b.comb[s].at[0], pair(b.rs_sem, s, 4), to_nxt),
            remote(b.relay[s].at[1], b.comb[s].at[1], pair(b.rs_sem, s, 5), to_prv),
        ]

    def combine(s):
        relays, combs = relay_out(s), comb_out(s)
        for h, q in ((0, 2 * nxt), (1, 2 * prv + 1)):
            relays[h].wait_recv()
            b.relay[s][h] += b.dense[s][pl.ds(pl.multiple_of(8 * q, 8), 8)]
            combs[h].start()

    def gather_copy(s, h, d):
        part = b.piece[s].at[column(layer, h)]
        return remote(part, part, pair(b.ag_sem, s, h, d), to_nxt if d == 0 else to_prv)

    def gather_pass(s, d):
        part = b.piece[s].at[column(prv if d == 0 else nxt, d)]
        return remote(part, part, pair(b.fw_sem, s, d), to_nxt if d == 0 else to_prv)

    def top_copy(s, h, d):
        part = b.top[s].at[column(layer, h)]
        device = (layer, up_row if d == 0 else down_row, col)
        return remote(part, part, (b.top_sem.at[d, s, h], b.top_sem.at[2, s, h]), device)

    def top_other(s, h, k):
        part = b.top[s].at[column(layer, h)]
        return remote(part, part, pair(b.tx_sem, s, h, k), other(k))

    onward = jnp.logical_and(row >= 1, row <= 3)
    backward = row >= 6

    def left_part(s, q, c):
        return b.left[s].at[q, pl.ds(pl.multiple_of((c % 2) * 4, 4), 4)]

    def left_row(s, k):
        c = (col + k) % GRID
        part = left_part(s, layer, c)
        return remote(part, part, (b.ly_sem.at[s, k], b.ly_sem.at[s, 0]), (layer, row, c))

    def left_row_wait(s):
        part = left_part(s, layer, col)
        op = remote(part, part, (b.ly_sem.at[s, 1], b.ly_sem.at[s, 0]), (layer, row, (col + 1) % GRID))
        op.wait_recv()

    def left_other(s, k):
        part = left_part(s, layer, col)
        return remote(part, part, pair(b.lx_sem, s, k), other(k))

    def left_core(s, k):
        part = left_part(s, (layer + k) % LAYERS, col)
        return remote(part, part, pair(b.lc_sem, s, k), sibling)

    def halves(action):
        action(1)
        pl.when(inner)(lambda: action(0))

    def reduce(s):
        plains, combs = plain_out(s), comb_out(s)
        n = THINS[s]

        def value(h, k):
            return b.sep_buf[h, pl.ds(k * BLOCK + STARTS[s], n)] - (
                b.dense[s][8 * (2 * layer + h) + k] + b.plain[s][h, k] + b.comb[s][h, k]
            )

        for h in range(2):
            plains[h].wait_recv()
            combs[h].wait_recv()
        for k in range(8):
            b.piece[s][column(layer, 1), k] = value(1, k)

        @pl.when(inner)
        def _():
            for k in range(8):
                b.piece[s][2 * layer, k] = value(0, k)

        @pl.when(edge)
        def _():
            for k in range(8):
                b.left[s][layer, k] = value(0, k)

        @pl.when(head)
        def _():
            def keep(h):
                b.top[s][column(layer, h)] = b.piece[s][column(layer, h), pl.ds(0, 4)]

            halves(keep)

        @pl.when(inner)
        def _():
            gather_copy(s, 0, 0).start()
            gather_copy(s, 0, 1).start()

        gather_copy(s, 1, 1).start()
        gather_copy(s, 1, 0).start()

    def top_out(s):
        @pl.when(head)
        def _():
            def send(h):
                top_copy(s, h, 0).start()
                top_copy(s, h, 1).start()

            halves(send)

    def pass_top(s):
        @pl.when(jnp.logical_not(head))
        def _():
            def onwards(h):
                top_copy(s, h, 0).wait_recv()

                @pl.when(onward)
                def _():
                    top_copy(s, h, 0).start()

                @pl.when(backward)
                def _():
                    top_copy(s, h, 1).start()

            halves(onwards)

        def to_others(h):
            for k in (1, 3, 2):
                top_other(s, h, k).start()

        halves(to_others)

    def slice_sent(s):
        def sent(k, carry):
            slice_copy(k, s).wait_send()
            return carry

        lax.fori_loop(1, OWNERS, sent, 0)

    def left_out(s):
        @pl.when(edge)
        def _():
            for k in (2, 6, 3, 7, 4, 5, 1):
                left_row(s, k).start()

    def pass_left(s):
        @pl.when(inner)
        def _():
            left_row_wait(s)

        for k in (1, 3, 2):
            left_other(s, k).start()

        @pl.when(col != 1)
        def _():
            left_core(s, 0).start()

    def pass_core(s):
        for k in (1, 3, 2):
            left_other(s, k).wait_recv()
            left_core(s, LAYERS - k).start()

    def pass_on(s):
        @pl.when(inner)
        def _():
            gather_copy(s, 0, 0).wait_recv()
            gather_pass(s, 0).start()

        gather_copy(s, 1, 1).wait_recv()
        gather_pass(s, 1).start()

    def lower_panel(s):
        n = THINS[s]

        @pl.when(inner)
        def _():
            left_core(s, 0).wait_recv()

        for k in range(1, LAYERS):
            left_core(s, k).wait_recv()
        rows = []
        for q in range(LAYERS):
            for i2 in range(2):
                rows.append(jnp.concatenate([b.left[s][q, 2 * j + i2] for j in range(4)], axis=1))
        hi, lo = split(jnp.concatenate(rows, axis=0))
        lower = dot(hi, b.inv_u[...]) + dot(lo, b.inv_u[...])
        b.low[s][...] = lower
        hi, lo = split(lower)
        b.low_hi[s][...] = hi
        b.low_lo[s][...] = lo

    def upper_panel(s):
        n = THINS[s]

        def arrived(h):
            for k in (1, 3, 2):
                top_other(s, h, k).wait_recv()

        halves(arrived)

        def add(c, carry):
            at = pl.ds(pl.multiple_of(c * 256, 256), 256)
            strips = [b.top[s][2 * c + h].reshape(4 * n, BLOCK) for h in range(2)]
            hi, lo = split(jnp.concatenate(strips, axis=1))
            inv = b.inv_lp[:, pl.ds(4 * STARTS[s], 4 * n)]
            term = dot(inv, hi) + dot(inv, lo)
            if s == 0:
                b.up[:, at] = term
            elif s < SLICES - 1:
                b.up[:, at] += term
            else:
                total = b.up[:, at] + term
                b.up[:, at] = total
                hi, lo = split(total)
                b.up_hi[:, at] = hi
                b.up_lo[:, at] = lo
            return carry

        lax.fori_loop(0, 4, add, 0)

    spread_extras(0)
    for s in range(SLICES):
        for k in range(LAYERS):
            core_copy(s, k).wait_recv()

        def slice_wait(k, carry):
            slice_copy(k, s).wait_recv()
            return carry

        lax.fori_loop(1, OWNERS, slice_wait, 0)
        add_up(s)
        for op in relay_out(s) + plain_out(s):
            op.start()
        if s == 0:

            @pl.when(inner)
            def _():
                sep_whole(0).wait()

            @pl.when(edge)
            def _():
                for j in range(4):
                    sep_edge(j).wait()

            sep_whole(1).wait()
        if s + AHEAD < SLICES:
            send_slice(s + AHEAD)
        if s + 1 < SLICES:
            spread_extras(s + 1)
        last = s == SLICES - 1
        if last:
            for t in range(s):
                top_out(t)
                left_out(t)
        if s >= 1:
            pass_on(s - 1)
        combine(s)
        if s >= 1:
            slice_sent(s - 1)
        if last:
            for t in range(s):
                pass_top(t)
            for t in range(s):
                pass_left(t)
        reduce(s)
        if last:
            top_out(s)
            left_out(s)
    slice_sent(SLICES - 1)
    pass_top(SLICES - 1)
    for s in range(SLICES - 1):
        pass_core(s)
    pass_on(SLICES - 1)
    pass_left(SLICES - 1)
    for s in range(SLICES - 1):
        lower_panel(s)
        upper_panel(s)
    pass_core(SLICES - 1)
    lower_panel(SLICES - 1)
    upper_panel(SLICES - 1)

    def out_copy(s):
        return [
            pltpu.make_async_copy(
                b.result[s].at[i], out_ref.at[pl.ds(i * BLOCK + STARTS[s], THINS[s])], b.out_sem.at[s, i]
            )
            for i in range(8)
        ]

    @pl.when(jnp.logical_and(edge, head))
    def _():
        rows = []
        for s in range(SLICES):
            for q in range(2):
                for i2 in range(2):
                    rows.append(jnp.concatenate([b.left[s][q, 2 * j + i2] for j in range(4)], axis=1))
        whole = jnp.concatenate(rows, axis=0)
        first, _ = split(whole)
        second, third = split(whole - first.astype(F32))
        order = b.perm[...].astype(F32).T.astype(BF16)
        b.up[:, 0:512] = dot(order, first) + dot(order, second) + dot(order, third)

    for s in range(SLICES):
        n = THINS[s]

        @pl.when(inner)
        def _():
            gather_copy(s, 0, 1).wait_recv()
            gather_pass(s, 0).wait_recv()

        gather_copy(s, 1, 0).wait_recv()
        gather_pass(s, 1).wait_recv()

        def trail(c, carry):
            at = pl.ds(pl.multiple_of(c * 256, 256), 256)
            hi, u_hi = b.low_hi[s][...], b.up_hi[:, at]
            change = dot(hi, u_hi) + (dot(b.low_lo[s][...], u_hi) + dot(hi, b.up_lo[:, at]))
            pieces = [b.piece[s][2 * c + h].reshape(8 * n, BLOCK) for h in range(2)]
            b.result[s][:, :, at] = (jnp.concatenate(pieces, axis=1) - change).reshape(8, n, 256)

            @pl.when(head)
            def _():
                for i in range(4):
                    b.result[s][i, :, at] = b.up[pl.ds(i * BLOCK + STARTS[s], n), at]

            return carry

        lax.fori_loop(0, 4, trail, 0)

        @pl.when(edge)
        def _():
            lower = b.low[s][...].reshape(8, n, 512)
            b.result[s][4:8, :, 0:512] = lower[4:8]

            @pl.when(jnp.logical_not(head))
            def _():
                b.result[s][0:4, :, 0:512] = lower[0:4]

        for op in out_copy(s):
            op.start()

    for s in range(SLICES):
        for op in relay_out(s) + plain_out(s) + comb_out(s):
            op.wait_send()
        for k in range(1, LAYERS):
            row_copy(s, k).wait_send()
            left_other(s, k).wait_send()
            left_core(s, k).wait_send()
        for k in range(LAYERS):
            core_copy(s, k).wait_send()

        @pl.when(col != 1)
        def _():
            left_core(s, 0).wait_send()

        @pl.when(edge)
        def _():
            for k in range(1, GRID):
                left_row(s, k).wait_send()

        def gone(h):
            @pl.when(jnp.logical_or(head, onward))
            def _():
                top_copy(s, h, 0).wait_send()

            @pl.when(jnp.logical_or(head, backward))
            def _():
                top_copy(s, h, 1).wait_send()

            for k in range(1, LAYERS):
                top_other(s, h, k).wait_send()
            for d in range(2):
                gather_copy(s, h, d).wait_send()
            gather_pass(s, h).wait_send()

        halves(gone)
    for h in range(1, 5):
        for op in ring_copies(h):
            op.wait_send()
    for k in range(1, LAYERS):
        peak_copy(k).wait()
        row_table(k).wait_send()
    for k in range(LAYERS):
        core_table(k).wait_send()
    peak_ref[...] = jnp.max(b.peak_buf[...], axis=0)
    for s in range(SLICES):
        for op in out_copy(s):
            op.wait()


def fused(owners, spots, left, right, separator, inverses, pivots):
    vmem = pl.BlockSpec(memory_space=pltpu.VMEM)
    hbm = pl.BlockSpec(memory_space=pl.ANY)
    return pl.pallas_call(
        fused_kernel,
        out_shape=(jax.ShapeDtypeStruct((8 * BLOCK, 1024), F32), jax.ShapeDtypeStruct((8, BLOCK), I32)),
        in_specs=[vmem, vmem, vmem, vmem, hbm, vmem, vmem],
        out_specs=(hbm, vmem),
        scratch_shapes=scratch_shapes(),
        compiler_params=pltpu.CompilerParams(
            collective_id=0, has_side_effects=True, vmem_limit_bytes=56 * 1024 * 1024
        ),
    )(owners, spots, left, right, separator, inverses, pivots)


def per_device(separator, left_factor, right_factor, owners, spots, pivot_order, panel_inverses):
    result, peak = fused(
        owners[:, 0][None, :], spots[None, :], left_factor, right_factor, separator, panel_inverses, pivot_order[None, :]
    )
    return lax.cond(
        peak[0, BLOCK - 1] > 1,
        lambda: general(separator, left_factor, right_factor, owners, spots, pivot_order, panel_inverses),
        lambda: result,
    )


def solution(mesh):
    in_specs = (
        P("prow", "pcol"),
        P(("layer", "prow", "pcol"), None, None),
        P(("layer", "prow", "pcol"), None, None),
        P(("layer", "prow", "pcol"), None),
        P(("layer", "prow", "pcol")),
        P(),
        P(),
    )
    return jax.shard_map(
        per_device, mesh=mesh, in_specs=in_specs, out_specs=P("prow", "pcol"), check_vma=False
    )
```
